32 devices in a mesh: req: 2 (over x), ctx: 16 (over z, y, core).
Axes of the slice: x: 2, y: 2, z: 4, core: 2. Of those that a mesh axis runs over, the one named last changes fastest.
Arguments:
- hidden: bfloat16 [512, 8192], P(('req', 'ctx')), parts along dimension 0, may hold values from -6 to 6
- keep_order: int32 [32, 16], P('req'), parts along dimension 0, may hold values from 0 to 15, each once within a row
- keep_count: int32 [32], P('req'), parts along dimension 0, may hold values from 1 to 4, 32 in all
- positions: int32 [512], P('req'), parts along dimension 0, may hold values from 130561 to 131071, as said below
- w_query: bfloat16 [8192, 8192], P(None, 'ctx'), may hold values from -0.0625 to 0.0625
- w_keyval: bfloat16 [8192, 2048], P(None, 'ctx'), may hold values from -0.25 to 0.25
- cache: bfloat16 [32768, 2048], P(('req', 'ctx')), parts along dimension 0, may hold values from -520 to 520, as said below
Outputs:
- attended: bfloat16 [64, 8192], P('req', 'ctx'), parts along dimension 0
The draws below stay inside these ranges and needn't reach their ends.
There are 2 independent parts, one for each index of `req`. The reference program is written for one: setup_inputs(seed, part) draws one part's arguments, and reference() takes and returns one part's arrays. A program takes and returns all parts, laid end to end along the dimension named above; an argument that names none is the same for every part. Nothing has to cross between parts.
Inputs may be any that keep to these rules, and one draw needn't show every extreme that they name: `keep_order`: each row lists every local index once; a shard's first keep_count entries are its kept tokens. `keep_count`: the counts sum to 32. `positions`: rising by 1 or 2 from token to token; the last token has position 131071. `cache`: keys are already rotated.
All inputs are finite; a program needn't handle non-finite values.
Results may differ from the reference program's by a relative error of at most 0.018.
The reference program's roundings to bfloat16 on the way (of `rows`, `query`, `keyval`, `new_keys` and `weights`) count: a program that leaves them out, or rounds other values in their place, can miss the bound.
Values may be sent and summed in bfloat16 or wider, within the bound.
A program may use at most 64 MiB of HBM per device.

```python
import math
import jax
import jax.numpy as jnp
import numpy as np
from jax import lax

D = 8192
H = 64
KVH = 8
HD = 128
SPAN_DEV = 16
KMAX = 4
KEEP = 32
SPAN = 256
CACHE = 16384
N_CTX = 16


def draw_positions(key, part):
    key = jax.random.fold_in(key, 11)
    gaps = jax.random.randint(key, (SPAN,), 1, 3, dtype=jnp.int32)
    after = jnp.cumsum(gaps[::-1])[::-1] - gaps
    return (131071 - after).astype(jnp.int32)


def draw_cache(key, part):
    key = jax.random.fold_in(key, 7)
    key_part, value_part = jax.random.split(key, 2)
    width = KVH * HD
    keys = jnp.clip(jax.random.normal(key_part, (CACHE, width), jnp.float32), -6.0, 6.0) * 3.0
    values = jnp.clip(jax.random.normal(value_part, (CACHE, width), jnp.float32), -6.0, 6.0)
    return jnp.concatenate([keys, values], axis=1).astype(jnp.bfloat16)


def shard_levels(own_key, dims, pieces, least, top_value):
    level = 1.0
    for axis_at, blocks in pieces:
        steps = jax.random.uniform(jax.random.fold_in(jax.random.fold_in(own_key, 6), axis_at), (blocks,), jnp.float32, least / len(pieces), top_value / len(pieces))
        level = level * jnp.repeat(jnp.exp(steps), dims[axis_at] // blocks).reshape((-1,) + (1,) * (len(dims) - 1 - axis_at))
    return level


def profile(amount, total, most, skew):
    weights = [(1 << 20) // math.isqrt(standing ** skew) + 1 for standing in range(2, amount + 1)]
    spare, given = total - most - (amount - 1), [1] * (amount - 1)
    while spare > 0:
        free = [i for i in range(amount - 1) if given[i] < most]
        mass, budget = sum([weights[i] for i in free]), spare
        for i in free:
            addition = min(most - given[i], max(1, budget * weights[i] // mass), spare)
            given[i] = given[i] + addition
            spare = spare - addition
    return np.array([most] + given)


def ragged(key, number_of, total, limit, slope):
    if number_of == 2:
        one = jax.random.randint(key, (), max(1, total - limit), min(limit, total - 1) + 1)
        return jnp.stack([one, total - one])
    lengths = jnp.asarray(profile(number_of, total, limit, slope), jnp.int32)
    couples = (number_of - 1) // 2
    source_of, sink = lengths[1:1 + 2 * couples:2], lengths[2:2 + 2 * couples:2]
    margin = jnp.minimum(source_of - 1, limit - sink)
    moved = jax.random.randint(jax.random.fold_in(key, 1), (couples,), 0, 1 << 20) % (margin + 1)
    lengths = lengths.at[1:1 + 2 * couples:2].set(source_of - moved).at[2:2 + 2 * couples:2].set(sink + moved)
    return lengths[jax.random.permutation(jax.random.fold_in(key, 2), number_of)]


def noise(rng, extent, scale, limit, cuts=(), kind=jnp.bfloat16):
    values = scale * jax.random.normal(rng, extent, jnp.float32)
    if cuts:
        values = values * shard_levels(rng, extent, cuts, -0.22, 0.18)
    return jnp.clip(values, -limit, limit).astype(kind)


def setup_inputs(seed: int = 0, part: int = 0) -> dict:
    seeds = jax.random.split(jax.random.key(seed), 8)
    part_keys = jax.random.split(jax.random.fold_in(seeds[7], part), 8)
    hidden = noise(part_keys[0], (SPAN, D), 1.0, 6.0, ((0, 16),))
    keep_order = jax.vmap(lambda own: jax.random.permutation(own, SPAN_DEV))(jax.random.split(part_keys[1], N_CTX)).reshape((N_CTX, SPAN_DEV)).astype(jnp.int32)
    keep_count = ragged(part_keys[2], N_CTX, KEEP, KMAX, 2).astype(jnp.int32)
    positions = draw_positions(jax.random.fold_in(jax.random.fold_in(seeds[7], part), 71), part)
    w_query = noise(seeds[4], (D, H * HD), D ** -0.5, 0.0625, ((1, 16),))
    w_keyval = noise(seeds[5], (D, 2 * KVH * HD), (D // 16) ** -0.5, 0.25, ((1, 16),))
    cache = draw_cache(jax.random.fold_in(jax.random.fold_in(seeds[7], part), 71), part)
    return dict(hidden=hidden, keep_order=keep_order, keep_count=keep_count, positions=positions, w_query=w_query, w_keyval=w_keyval, cache=cache)


def rope_table(head_size):
    half = head_size // 2
    period = 2.0 * math.pi
    scaled_list = []
    wrapped_list = []
    for column in range(half):
        inverse = 500000.0 ** (-2.0 * column / head_size)
        wavelen = 2.0 * math.pi / inverse
        if wavelen > 8192.0:
            scaled_rate = inverse / 8.0
        elif wavelen < 2048.0:
            scaled_rate = inverse
        else:
            smooth = (8192.0 / wavelen - 1.0) / 3.0
            scaled_rate = (1.0 - smooth) * inverse / 8.0 + smooth * inverse
        scaled_list.append(scaled_rate)
        step_angle = 1024.0 * scaled_rate
        wrapped_list.append(step_angle - period * (step_angle // period))
    return (jnp.asarray(scaled_list, jnp.float32), jnp.asarray(wrapped_list, jnp.float32))

def rotate(values, places):
    scaled, wrapped = rope_table(values.shape[-1])
    upper = (places // 1024).astype(jnp.float32)
    lower = (places % 1024).astype(jnp.float32)
    angle = lower[:, None] * scaled[None, :] + upper[:, None] * wrapped[None, :]
    cosine = jnp.cos(angle)[:, None, :]
    sine = jnp.sin(angle)[:, None, :]
    half = values.shape[-1] // 2
    first = values[..., :half]
    second = values[..., half:]
    return jnp.concatenate([first * cosine - second * sine, second * cosine + first * sine], axis=-1)

def kept_sources(keep_count, kept_total, shards):
    ends = jnp.cumsum(keep_count).astype(jnp.int32)
    starts = ends - keep_count
    slots = jnp.arange(kept_total, dtype=jnp.int32)
    owner = lax.optimization_barrier(jnp.sum((ends[None, :] <= slots[:, None]).astype(jnp.int32), axis=1)).astype(jnp.int32)
    ids = jnp.arange(shards, dtype=jnp.int32)
    first = lax.optimization_barrier(jnp.sum(jnp.where(ids[None, :] == owner[:, None], starts[None, :], 0), axis=1)).astype(jnp.int32)
    return (owner, slots - first)

def reference(hidden, keep_order, keep_count, positions, w_query, w_keyval, cache):
    owner, local = kept_sources(keep_count, KEEP, N_CTX)
    source = (owner * SPAN_DEV + keep_order[owner, local]).astype(jnp.int32)
    rows = hidden[source]
    places = positions[source]
    query = jnp.dot(rows, w_query, preferred_element_type=jnp.float32).reshape(KEEP, H, HD)
    query = rotate(query, places).astype(jnp.bfloat16)
    keyval = jnp.dot(rows, w_keyval, preferred_element_type=jnp.float32).astype(jnp.bfloat16)
    new_keys = rotate(keyval[:, :KVH * HD].astype(jnp.float32).reshape(KEEP, KVH, HD), places).astype(jnp.bfloat16)
    new_vals = keyval[:, KVH * HD:].reshape(KEEP, KVH, HD)
    keys = jnp.concatenate([cache[:, :KVH * HD].reshape(CACHE, KVH, HD), new_keys], axis=0)
    vals = jnp.concatenate([cache[:, KVH * HD:].reshape(CACHE, KVH, HD), new_vals], axis=0)
    visible = jnp.concatenate([jnp.ones((KEEP, CACHE), bool), places[None, :] <= places[:, None]], axis=1)
    scale = 1.0 / math.sqrt(HD)

    def one_head(head):
        group = head // (H // KVH)
        q_head = lax.dynamic_index_in_dim(query, head, 1, False)
        k_head = lax.dynamic_index_in_dim(keys, group, 1, False)
        v_head = lax.dynamic_index_in_dim(vals, group, 1, False)
        scores = jnp.dot(q_head, k_head.T, preferred_element_type=jnp.float32) * scale
        scores = jnp.where(visible, scores, -1e+30)
        top = lax.optimization_barrier(jnp.max(scores, axis=1, keepdims=True))
        weights = jnp.exp(scores - top)
        total = lax.optimization_barrier(jnp.sum(weights, axis=1, keepdims=True))
        numer = jnp.dot(weights.astype(jnp.bfloat16), v_head, preferred_element_type=jnp.float32)
        return (numer / total).astype(jnp.bfloat16)
    heads = lax.map(one_head, jnp.arange(H, dtype=jnp.int32))
    return jnp.transpose(heads, (1, 0, 2)).reshape(KEEP, H * HD)
```

```python
import functools
import math

import jax
import jax.numpy as jnp
from jax import lax
from jax.experimental import pallas as pl
from jax.experimental.pallas import tpu as pltpu
from jax.sharding import PartitionSpec as P

H = 64
KVH = 8
HD = 128
KEEP_DEV = 2
KMAX = 4


def rope_table(head_size):
    half = head_size // 2
    period = 2.0 * math.pi
    scaled_list = []
    wrapped_list = []
    for column in range(half):
        inverse = 500000.0 ** (-2.0 * column / head_size)
        wavelen = 2.0 * math.pi / inverse
        if wavelen > 8192.0:
            scaled_rate = inverse / 8.0
        elif wavelen < 2048.0:
            scaled_rate = inverse
        else:
            smooth = (8192.0 / wavelen - 1.0) / 3.0
            scaled_rate = (1.0 - smooth) * inverse / 8.0 + smooth * inverse
        scaled_list.append(scaled_rate)
        step_angle = 1024.0 * scaled_rate
        wrapped_list.append(step_angle - period * (step_angle // period))
    return (jnp.asarray(scaled_list, jnp.float32), jnp.asarray(wrapped_list, jnp.float32))


def rotate(values, places):
    scaled, wrapped = rope_table(values.shape[-1])
    upper = (places // 1024).astype(jnp.float32)
    lower = (places % 1024).astype(jnp.float32)
    angle = lower[:, None] * scaled[None, :] + upper[:, None] * wrapped[None, :]
    cosine = jnp.cos(angle)[:, None, :]
    sine = jnp.sin(angle)[:, None, :]
    half = values.shape[-1] // 2
    first = values[..., :half]
    second = values[..., half:]
    return jnp.concatenate(
        [first * cosine - second * sine, second * cosine + first * sine], axis=-1
    )


def kept_sources(keep_count, kept_total, shards):
    ends = jnp.cumsum(keep_count)
    starts = ends - keep_count
    slots = jnp.arange(kept_total, dtype=jnp.int32)
    owner = jnp.sum((ends[None, :] <= slots[:, None]).astype(jnp.int32), axis=1)
    ids = jnp.arange(shards, dtype=jnp.int32)
    first = jnp.sum(jnp.where(ids[None, :] == owner[:, None], starts[None, :], 0), axis=1)
    return (owner, slots - first)


def body(hidden, keep_order, keep_count, positions, w_query, w_keyval, cache):
    shards = lax.axis_size("ctx")
    me = lax.axis_index("ctx")
    span_rows = hidden.shape[0]
    kept_total = KEEP_DEV * shards
    block = KEEP_DEV
    cache_rows = cache.shape[0]
    heads_here = H // shards
    order_here = lax.dynamic_slice_in_dim(keep_order, me, 1, 0)[0, :KMAX]
    slot_rows = hidden[order_here]
    rows_all = lax.all_gather(slot_rows, "ctx", axis=0, tiled=True)
    owner, local = kept_sources(keep_count, kept_total, shards)
    rows = rows_all[owner * KMAX + local]
    places = positions[owner * span_rows + keep_order[owner, local]]
    query = jnp.dot(rows, w_query, preferred_element_type=jnp.float32).reshape(
        kept_total, heads_here, HD
    )
    query = rotate(query, places).astype(jnp.bfloat16).reshape(kept_total, heads_here * HD)
    key_part = jnp.dot(rows, w_keyval, preferred_element_type=jnp.float32).astype(jnp.bfloat16)
    own_keyval = lax.all_to_all(key_part, "ctx", split_axis=0, concat_axis=1, tiled=True)
    own_places = lax.dynamic_slice_in_dim(places, me * block, block, 0)
    new_keys = rotate(
        own_keyval[:, : KVH * HD].astype(jnp.float32).reshape(block, KVH, HD), own_places
    )
    new_keys = new_keys.astype(jnp.bfloat16).reshape(block, KVH * HD)
    keys = jnp.concatenate([cache[:, : KVH * HD], new_keys], axis=0)
    values = jnp.concatenate([cache[:, KVH * HD :], own_keyval[:, KVH * HD :]], axis=0)
    queries = lax.all_gather(query, "ctx", axis=1, tiled=True)
    visible = jnp.concatenate(
        [jnp.ones((kept_total, cache_rows), bool), own_places[None, :] <= places[:, None]], axis=1
    )
    group = H // KVH
    scale = 1.0 / math.sqrt(HD)
    numer_list = []
    top_list = []
    total_list = []
    for index in range(KVH):
        q_group = queries[:, index * group * HD : (index + 1) * group * HD].reshape(
            kept_total, group, HD
        )
        k_group = keys[:, index * HD : (index + 1) * HD]
        v_group = values[:, index * HD : (index + 1) * HD]
        scores = (
            jnp.einsum("qhd,kd->qhk", q_group, k_group, preferred_element_type=jnp.float32) * scale
        )
        scores = jnp.where(visible[:, None, :], scores, -1e30)
        top = jnp.max(scores, axis=2)
        weights = jnp.exp(scores - top[..., None])
        total_list.append(jnp.sum(weights, axis=2))
        top_list.append(top)
        numer = jnp.einsum(
            "qhk,kd->qhd", weights.astype(jnp.bfloat16), v_group, preferred_element_type=jnp.float32
        )
        numer_list.append(numer.reshape(kept_total, group * HD))
    numer = jnp.concatenate(numer_list, axis=1)
    top = jnp.concatenate(top_list, axis=1)
    total = jnp.concatenate(total_list, axis=1)
    best = lax.pmax(top.astype(jnp.bfloat16), "ctx").astype(top.dtype)
    factor = jnp.exp(top - best)
    scaled_numer = (numer.reshape(kept_total, H, HD) * factor[..., None]).reshape(
        kept_total, H * HD
    )
    result, denom = (
        lax.psum_scatter(scaled_numer, "ctx", scatter_dimension=1, tiled=True),
        lax.psum_scatter(total * factor, "ctx", scatter_dimension=1, tiled=True),
    )
    result = result.reshape(kept_total, heads_here, HD)
    return (result / denom[..., None]).reshape(kept_total, heads_here * HD).astype(jnp.bfloat16)


MESH = pl.DeviceIdType.MESH
ZS = 4
SHARDS = 16
KEEP = 32
GROUPS = 4
WIDE = 2048
QROWS = 128
EXP2_SCALE = math.log2(math.e) / math.sqrt(HD)
MSG = QROWS + 16


def pack(ref, index, partial, lse):
    ref[index, :QROWS, :] = partial.astype(jnp.bfloat16)
    high = lse.astype(jnp.bfloat16).astype(jnp.float32)
    middle = (lse - high).astype(jnp.bfloat16).astype(jnp.float32)
    low = lse - high - middle
    row = lax.broadcasted_iota(jnp.int32, (16, QROWS), 0)
    stats = jnp.where(row == 0, high, jnp.where(row == 1, middle, jnp.where(row == 2, low, 0.0)))
    ref[index, QROWS:, :] = stats.astype(jnp.bfloat16)


def unpack(ref, index):
    stats = ref[index, QROWS:, :].astype(jnp.float32)
    return ref[index, :QROWS, :].astype(jnp.float32), jnp.sum(stats, axis=0, keepdims=True)


def merge(pieces):
    best = functools.reduce(jnp.maximum, [lse for _, lse in pieces])
    factors = [jnp.exp2(lse - best) for _, lse in pieces]
    total = sum(factors)
    inverse = 1.0 / total
    mixed = sum(partial * (factor * inverse) for (partial, _), factor in zip(pieces, factors))
    return mixed, best + jnp.log2(total)


def contract(a, b, dims):
    return lax.dot_general(a, b, ((dims[:1], dims[1:]), ((), ())), preferred_element_type=jnp.float32)


def kernel(
    order, count, pos, table, hidden, w_query, w_keyval, cache, out,
    hidden_v, query_v, keyval_v, cache_v, slots, qbuf, values_t,
    own, own_lse, send_s, recv_s, send_y, recv_y, send_z, recv_z,
    load_sem, row_send, row_recv, q_send, q_recv,
    s_send, s_recv, y_send, y_recv, z_send, z_recv,
):
    me = lax.axis_index("ctx")
    z = me // 4
    y = (me // 2) % 2
    c = me % 2
    sibling = me + 1 - 2 * c
    y_peer = me + 2 - 4 * y

    def z_at(dz):
        return (z + dz) % ZS

    def z_peer(dz):
        return z_at(dz) * 4 + me % 4

    def block_at(dz, dy, dc):
        yy = y if dy == 0 else 1 - y
        cc = c if dc == 0 else 1 - c
        return z_at(dz) * 4 + yy * 2 + cc

    loads = [
        pltpu.make_async_copy(hidden, hidden_v, load_sem.at[0]),
        pltpu.make_async_copy(w_query, query_v, load_sem.at[1]),
        pltpu.make_async_copy(w_keyval, keyval_v, load_sem.at[2]),
        pltpu.make_async_copy(cache, cache_v, load_sem.at[3]),
    ]
    for load in loads:
        load.start()

    barrier = pltpu.get_barrier_semaphore()
    peers = [sibling, y_peer] + [z_peer(dz) for dz in (1, 2, 3)]
    for peer in peers:
        pl.semaphore_signal(barrier, inc=1, device_id={"ctx": peer}, device_id_type=MESH)

    row = lax.broadcasted_iota(jnp.int32, (16, 16), 0)
    column = lax.broadcasted_iota(jnp.int32, (16, 16), 1)
    chosen = jnp.zeros((16, 16), jnp.int32)
    for slot in range(KMAX):
        chosen = jnp.where(row % 4 == slot, order[me, slot], chosen)
    loads[0].wait()
    picked = jnp.zeros((16, WIDE), jnp.float32)
    for g in range(GROUPS):
        onehot = jnp.where((chosen == column) & (row // 4 == g), 1.0, 0.0).astype(jnp.bfloat16)
        picked += contract(onehot, hidden_v[:, g * WIDE : (g + 1) * WIDE], (1, 0))
    slots[me] = picked.astype(jnp.bfloat16)
    pl.semaphore_wait(barrier, len(peers))

    def relay(buf, send_sem, recv_sem, between):
        sent = []

        def send(at, receiver_at, peer):
            copy = pltpu.make_async_remote_copy(
                src_ref=buf.at[block_at(*at)],
                dst_ref=buf.at[block_at(*at)],
                send_sem=send_sem.at[len(sent)],
                recv_sem=recv_sem.at[receiver_at],
                device_id={"ctx": peer},
                device_id_type=MESH,
            )
            copy.start()
            sent.append(copy)

        def arrived(dz, dy, dc):
            pltpu.make_async_remote_copy(
                src_ref=buf.at[block_at(dz, dy, dc)],
                dst_ref=buf.at[block_at(dz, dy, dc)],
                send_sem=send_sem.at[0],
                recv_sem=recv_sem.at[dz * 4 + dy * 2 + dc],
                device_id={"ctx": sibling},
                device_id_type=MESH,
            ).wait_recv()

        for dz in (2, 1, 3):
            send((0, 0, 0), (ZS - dz) * 4, z_peer(dz))
        send((0, 0, 0), 2, y_peer)
        send((0, 0, 0), 1, sibling)
        result = between()
        for dz in (1, 3, 2):
            arrived(dz, 0, 0)
            send((dz, 0, 0), dz * 4 + 2, y_peer)
            send((dz, 0, 0), dz * 4 + 1, sibling)
        for dz in (0, 1, 3, 2):
            arrived(dz, 1, 0)
            send((dz, 1, 0), dz * 4 + 3, sibling)
        for dy in (0, 1):
            for dz in (0, 1, 3, 2):
                arrived(dz, dy, 1)
        return sent, result

    def tables():
        lane = lax.broadcasted_iota(jnp.int32, (1, 256), 1)
        source = lane // 16
        local = lane % 4
        first = jnp.zeros((1, 256), jnp.int32)
        kept = jnp.zeros((1, 256), jnp.int32)
        place = jnp.zeros((1, 256), jnp.int32)
        begin = jnp.int32(0)
        for s in range(SHARDS):
            first = jnp.where(source == s, begin, first)
            kept = jnp.where(source == s, count[s], kept)
            begin = begin + count[s]
            for slot in range(KMAX):
                place = jnp.where(
                    (source == s) & (local == slot), pos[s * 16 + order[s, slot]], place
                )
        target = jnp.where(local < kept, first + local, -1)
        listed = lax.broadcasted_iota(jnp.int32, (KEEP, 256), 0) == target
        group = (lane // 4) % 4
        picks = [
            jnp.where(listed & (group == g), 1.0, 0.0).astype(jnp.bfloat16) for g in range(GROUPS)
        ]
        mine = jnp.where(listed & (group == 0), 1.0, 0.0)
        upper = jnp.sum(mine * (place >> 10).astype(jnp.float32), axis=1, keepdims=True)
        lower = jnp.sum(mine * (place & 1023).astype(jnp.float32), axis=1, keepdims=True)
        angle = lower * table[0:1, :] + upper * table[1:2, :]
        return picks, upper * 1024.0 + lower, jnp.cos(angle), jnp.sin(angle) * table[2:3, :]

    def before_rows():
        result = tables()
        loads[3].wait()
        return result

    row_sent, (picks, places, cosine, sine) = relay(slots, row_send, row_recv, before_rows)
    loads[1].wait()
    loads[2].wait()
    query = jnp.zeros((KEEP, 4 * HD), jnp.float32)
    keyval = jnp.zeros((KEEP, HD), jnp.float32)
    for g in range(GROUPS):
        rows = contract(picks[g], slots[...].reshape(256, WIDE), (1, 0)).astype(jnp.bfloat16)
        query += contract(rows, query_v[g * WIDE : (g + 1) * WIDE, :], (1, 0))
        keyval += contract(rows, keyval_v[g * WIDE : (g + 1) * WIDE, :], (1, 0))

    def turn(part):
        return part * cosine + pltpu.roll(part, HD // 2, 1) * sine

    for h in range(4):
        qbuf[me, h * KEEP : (h + 1) * KEEP, :] = turn(query[:, h * HD : (h + 1) * HD]).astype(
            jnp.bfloat16
        )
    plain = keyval.astype(jnp.bfloat16).astype(jnp.float32)
    qbuf[me, QROWS:, :] = jnp.where(me < KVH, turn(plain), plain).astype(jnp.bfloat16)

    def before_queries():
        for g in range(KVH):
            at = (KVH + g) * HD
            values_t[g] = cache_v[:, at : at + HD].T

    q_sent, _ = relay(qbuf, q_send, q_recv, before_queries)

    def attend(g):
        keys = cache_v[:, pl.ds(pl.multiple_of(g * HD, HD), HD)]
        both = jnp.concatenate(
            [qbuf[2 * g + 1 - c, :QROWS, :], qbuf[2 * g + c, :QROWS, :]], axis=0
        )
        scores = contract(keys, both, (1, 1))
        top = jnp.max(scores, axis=0, keepdims=True)
        weights = jnp.exp2((scores - top) * EXP2_SCALE)
        total = jnp.sum(weights, axis=0, keepdims=True)
        numer = contract(values_t[g], weights.astype(jnp.bfloat16), (1, 0))
        partial = numer * (1.0 / total)
        lse = top * EXP2_SCALE + jnp.log2(total)
        pack(send_s, g, partial[:, :QROWS], lse[:, :QROWS])
        own[g] = partial[:, QROWS:]
        own_lse[g] = jnp.broadcast_to(lse[:, QROWS:], (8, QROWS))

    def move(src, dst, index_from, index_to, ssem, rsem, peer):
        return pltpu.make_async_remote_copy(
            src_ref=src.at[index_from],
            dst_ref=dst.at[index_to],
            send_sem=ssem,
            recv_sem=rsem,
            device_id={"ctx": peer},
            device_id_type=MESH,
        )

    def to_sibling(dz, dy):
        g = z_at(dz) * 2 + (y if dy == 0 else 1 - y)
        at = dz * 2 + dy
        return move(send_s, recv_s, g, g, s_send.at[at], s_recv.at[at], sibling)

    def to_y(dz):
        return move(send_y, recv_y, dz, dz, y_send.at[dz], y_recv.at[dz], y_peer)

    def to_z(dz):
        return move(send_z, recv_z, dz, ZS - dz, z_send.at[dz], z_recv.at[ZS - dz], z_peer(dz))

    def mine_and_sibling(dz, dy):
        g = z_at(dz) * 2 + (y if dy == 0 else 1 - y)
        to_sibling(dz, dy).wait_recv()
        return [(own[g], own_lse[g, 0:1, :]), unpack(recv_s, g)]

    turns = [(dz, dy) for dz in (2, 1, 3, 0) for dy in (1, 0)]

    def follow(dz, dy):
        if dy == 1:
            pack(send_y, dz, *merge(mine_and_sibling(dz, 1)))
            to_y(dz).start()
            return None
        pieces = mine_and_sibling(dz, 0)
        to_y(dz).wait_recv()
        pieces.append(unpack(recv_y, dz))
        if dz == 0:
            return merge(pieces)
        pack(send_z, dz, *merge(pieces))
        to_z(dz).start()
        return None

    lag = 1
    local = None
    for step in range(len(turns) + lag):
        if step < len(turns):
            dz, dy = turns[step]
            attend(z_at(dz) * 2 + (y if dy == 0 else 1 - y))
            to_sibling(dz, dy).start()
        if step == len(turns) - 1:
            new_keys = qbuf[me // 2, QROWS:, :]
            new_values = qbuf[KVH + me // 2, QROWS:, :]
            spot = lax.broadcasted_iota(jnp.int32, (KEEP, QROWS), 0)
            lane = lax.broadcasted_iota(jnp.int32, (KEEP, QROWS), 1)
            asker = jnp.sum(jnp.where(lane % KEEP == spot, places, 0.0), axis=0, keepdims=True)
            scores = contract(new_keys, qbuf[me, :QROWS, :], (1, 1))
            seen = places <= asker
            scores = jnp.where(seen, scores, -1e30)
            top = jnp.max(scores, axis=0, keepdims=True)
            weights = jnp.where(seen, jnp.exp2((scores - top) * EXP2_SCALE), 0.0)
            total = jnp.sum(weights, axis=0, keepdims=True)
            numer = contract(new_values, weights.astype(jnp.bfloat16), (0, 0))
            fresh = (numer * (1.0 / total), top * EXP2_SCALE + jnp.log2(total))
        if step >= lag:
            local = follow(*turns[step - lag])

    pieces = [local, fresh]
    for dz in (1, 3, 2):
        pltpu.make_async_remote_copy(
            src_ref=send_z.at[dz],
            dst_ref=recv_z.at[dz],
            send_sem=z_send.at[dz],
            recv_sem=z_recv.at[dz],
            device_id={"ctx": z_peer(dz)},
            device_id_type=MESH,
        ).wait_recv()
        pieces.append(unpack(recv_z, dz))
    mixed, _ = merge(pieces)
    final = mixed.T
    for h in range(4):
        out[:, h * HD : (h + 1) * HD] = final[h * KEEP : (h + 1) * KEEP, :].astype(jnp.bfloat16)

    for copy in row_sent + q_sent:
        copy.wait_send()
    for dz, dy in turns:
        to_sibling(dz, dy).wait_send()
    for dz in range(ZS):
        to_y(dz).wait_send()
    for dz in (1, 2, 3):
        to_z(dz).wait_send()


def kernel_body(hidden, keep_order, keep_count, positions, w_query, w_keyval, cache):
    scaled, wrapped = rope_table(HD)
    sign = jnp.asarray([-1.0] * (HD // 2) + [1.0] * (HD // 2), jnp.float32)
    table = jnp.stack(
        [jnp.concatenate([scaled, scaled]), jnp.concatenate([wrapped, wrapped]), sign]
        + [jnp.zeros((HD,), jnp.float32)] * 5
    )
    smem = pl.BlockSpec(memory_space=pltpu.SMEM)
    vmem = pl.BlockSpec(memory_space=pltpu.VMEM)
    anywhere = pl.BlockSpec(memory_space=pl.ANY)
    tokens = cache.shape[0]
    bf16 = jnp.bfloat16
    dma = pltpu.SemaphoreType.DMA
    return pl.pallas_call(
        kernel,
        out_shape=jax.ShapeDtypeStruct((KEEP, 4 * HD), bf16),
        in_specs=[smem, smem, smem, vmem, anywhere, anywhere, anywhere, anywhere],
        out_specs=vmem,
        scratch_shapes=[
            pltpu.VMEM(hidden.shape, bf16),
            pltpu.VMEM(w_query.shape, bf16),
            pltpu.VMEM(w_keyval.shape, bf16),
            pltpu.VMEM(cache.shape, bf16),
            pltpu.VMEM((SHARDS, 16, WIDE), bf16),
            pltpu.VMEM((SHARDS, QROWS + KEEP, HD), bf16),
            pltpu.VMEM((KVH, HD, tokens), bf16),
            pltpu.VMEM((KVH, HD, QROWS), jnp.float32),
            pltpu.VMEM((KVH, 8, QROWS), jnp.float32),
            pltpu.VMEM((KVH, MSG, QROWS), bf16),
            pltpu.VMEM((KVH, MSG, QROWS), bf16),
            pltpu.VMEM((ZS, MSG, QROWS), bf16),
            pltpu.VMEM((ZS, MSG, QROWS), bf16),
            pltpu.VMEM((ZS, MSG, QROWS), bf16),
            pltpu.VMEM((ZS, MSG, QROWS), bf16),
            dma((4,)),
            dma((15,)),
            dma((16,)),
            dma((15,)),
            dma((16,)),
            dma((8,)),
            dma((8,)),
            dma((4,)),
            dma((4,)),
            dma((4,)),
            dma((4,)),
        ],
        compiler_params=pltpu.CompilerParams(
            collective_id=0, has_side_effects=True, vmem_limit_bytes=44 * 1024 * 1024
        ),
        cost_estimate=pl.CostEstimate(
            flops=1_500_000_000, bytes_accessed=15_000_000, transcendentals=2_100_000
        ),
    )(keep_order, keep_count, positions, table, hidden, w_query, w_keyval, cache)


def solution(mesh):
    use = kernel_body if mesh.shape["ctx"] == 16 else body
    return jax.shard_map(
        use,
        mesh=mesh,
        in_specs=(
            P(("req", "ctx"), None),
            P("req", None),
            P("req"),
            P("req"),
            P(None, "ctx"),
            P(None, "ctx"),
            P(("req", "ctx"), None),
        ),
        out_specs=P("req", "ctx"),
        check_vma=False,
    )
```

```python
import functools
import math

import jax
import jax.numpy as jnp
from jax import lax
from jax.experimental import pallas as pl
from jax.experimental.pallas import tpu as pltpu
from jax.sharding import PartitionSpec as P

H = 64
KVH = 8
HD = 128
KEEP_DEV = 2
KMAX = 4


def rope_table(head_size):
    half = head_size // 2
    period = 2.0 * math.pi
    scaled_list = []
    wrapped_list = []
    for column in range(half):
        inverse = 500000.0 ** (-2.0 * column / head_size)
        wavelen = 2.0 * math.pi / inverse
        if wavelen > 8192.0:
            scaled_rate = inverse / 8.0
        elif wavelen < 2048.0:
            scaled_rate = inverse
        else:
            smooth = (8192.0 / wavelen - 1.0) / 3.0
            scaled_rate = (1.0 - smooth) * inverse / 8.0 + smooth * inverse
        scaled_list.append(scaled_rate)
        step_angle = 1024.0 * scaled_rate
        wrapped_list.append(step_angle - period * (step_angle // period))
    return (jnp.asarray(scaled_list, jnp.float32), jnp.asarray(wrapped_list, jnp.float32))


def rotate(values, places):
    scaled, wrapped = rope_table(values.shape[-1])
    upper = (places // 1024).astype(jnp.float32)
    lower = (places % 1024).astype(jnp.float32)
    angle = lower[:, None] * scaled[None, :] + upper[:, None] * wrapped[None, :]
    cosine = jnp.cos(angle)[:, None, :]
    sine = jnp.sin(angle)[:, None, :]
    half = values.shape[-1] // 2
    first = values[..., :half]
    second = values[..., half:]
    return jnp.concatenate(
        [first * cosine - second * sine, second * cosine + first * sine], axis=-1
    )


def kept_sources(keep_count, kept_total, shards):
    ends = jnp.cumsum(keep_count)
    starts = ends - keep_count
    slots = jnp.arange(kept_total, dtype=jnp.int32)
    owner = jnp.sum((ends[None, :] <= slots[:, None]).astype(jnp.int32), axis=1)
    ids = jnp.arange(shards, dtype=jnp.int32)
    first = jnp.sum(jnp.where(ids[None, :] == owner[:, None], starts[None, :], 0), axis=1)
    return (owner, slots - first)


def body(hidden, keep_order, keep_count, positions, w_query, w_keyval, cache):
    shards = lax.axis_size("ctx")
    me = lax.axis_index("ctx")
    span_rows = hidden.shape[0]
    kept_total = KEEP_DEV * shards
    block = KEEP_DEV
    cache_rows = cache.shape[0]
    heads_here = H // shards
    order_here = lax.dynamic_slice_in_dim(keep_order, me, 1, 0)[0, :KMAX]
    slot_rows = hidden[order_here]
    rows_all = lax.all_gather(slot_rows, "ctx", axis=0, tiled=True)
    owner, local = kept_sources(keep_count, kept_total, shards)
    rows = rows_all[owner * KMAX + local]
    places = positions[owner * span_rows + keep_order[owner, local]]
    query = jnp.dot(rows, w_query, preferred_element_type=jnp.float32).reshape(
        kept_total, heads_here, HD
    )
    query = rotate(query, places).astype(jnp.bfloat16).reshape(kept_total, heads_here * HD)
    key_part = jnp.dot(rows, w_keyval, preferred_element_type=jnp.float32).astype(jnp.bfloat16)
    own_keyval = lax.all_to_all(key_part, "ctx", split_axis=0, concat_axis=1, tiled=True)
    own_places = lax.dynamic_slice_in_dim(places, me * block, block, 0)
    new_keys = rotate(
        own_keyval[:, : KVH * HD].astype(jnp.float32).reshape(block, KVH, HD), own_places
    )
    new_keys = new_keys.astype(jnp.bfloat16).reshape(block, KVH * HD)
    keys = jnp.concatenate([cache[:, : KVH * HD], new_keys], axis=0)
    values = jnp.concatenate([cache[:, KVH * HD :], own_keyval[:, KVH * HD :]], axis=0)
    queries = lax.all_gather(query, "ctx", axis=1, tiled=True)
    visible = jnp.concatenate(
        [jnp.ones((kept_total, cache_rows), bool), own_places[None, :] <= places[:, None]], axis=1
    )
    group = H // KVH
    scale = 1.0 / math.sqrt(HD)
    numer_list = []
    top_list = []
    total_list = []
    for index in range(KVH):
        q_group = queries[:, index * group * HD : (index + 1) * group * HD].reshape(
            kept_total, group, HD
        )
        k_group = keys[:, index * HD : (index + 1) * HD]
        v_group = values[:, index * HD : (index + 1) * HD]
        scores = (
            jnp.einsum("qhd,kd->qhk", q_group, k_group, preferred_element_type=jnp.float32) * scale
        )
        scores = jnp.where(visible[:, None, :], scores, -1e30)
        top = jnp.max(scores, axis=2)
        weights = jnp.exp(scores - top[..., None])
        total_list.append(jnp.sum(weights, axis=2))
        top_list.append(top)
        numer = jnp.einsum(
            "qhk,kd->qhd", weights.astype(jnp.bfloat16), v_group, preferred_element_type=jnp.float32
        )
        numer_list.append(numer.reshape(kept_total, group * HD))
    numer = jnp.concatenate(numer_list, axis=1)
    top = jnp.concatenate(top_list, axis=1)
    total = jnp.concatenate(total_list, axis=1)
    best = lax.pmax(top.astype(jnp.bfloat16), "ctx").astype(top.dtype)
    factor = jnp.exp(top - best)
    scaled_numer = (numer.reshape(kept_total, H, HD) * factor[..., None]).reshape(
        kept_total, H * HD
    )
    result, denom = (
        lax.psum_scatter(scaled_numer, "ctx", scatter_dimension=1, tiled=True),
        lax.psum_scatter(total * factor, "ctx", scatter_dimension=1, tiled=True),
    )
    result = result.reshape(kept_total, heads_here, HD)
    return (result / denom[..., None]).reshape(kept_total, heads_here * HD).astype(jnp.bfloat16)


MESH = pl.DeviceIdType.MESH
ZS = 4
SHARDS = 16
KEEP = 32
GROUPS = 4
WIDE = 2048
QROWS = 128
EXP2_SCALE = math.log2(math.e) / math.sqrt(HD)
MSG = QROWS + 16


def pack(ref, index, partial, lse):
    ref[index, :QROWS, :] = partial.astype(jnp.bfloat16)
    high = lse.astype(jnp.bfloat16).astype(jnp.float32)
    middle = (lse - high).astype(jnp.bfloat16).astype(jnp.float32)
    low = lse - high - middle
    row = lax.broadcasted_iota(jnp.int32, (16, QROWS), 0)
    stats = jnp.where(row == 0, high, jnp.where(row == 1, middle, jnp.where(row == 2, low, 0.0)))
    ref[index, QROWS:, :] = stats.astype(jnp.bfloat16)


def unpack(ref, index):
    stats = ref[index, QROWS:, :].astype(jnp.float32)
    return ref[index, :QROWS, :].astype(jnp.float32), jnp.sum(stats, axis=0, keepdims=True)


def merge(pieces):
    best = functools.reduce(jnp.maximum, [lse for _, lse in pieces])
    factors = [jnp.exp2(lse - best) for _, lse in pieces]
    total = sum(factors)
    inverse = 1.0 / total
    mixed = sum(partial * (factor * inverse) for (partial, _), factor in zip(pieces, factors))
    return mixed, best + jnp.log2(total)


def contract(a, b, dims):
    return lax.dot_general(a, b, ((dims[:1], dims[1:]), ((), ())), preferred_element_type=jnp.float32)


def kernel(
    order_h, count_h, pos_h, table_h, hidden, w_query, w_keyval, cache, out,
    order, count, pos, table, hidden_v, query_v, keyval_v, cache_v, slots, qbuf, values_t,
    own, own_lse, send_s, recv_s, send_y, recv_y, send_z, recv_z,
    load_sem, row_send, row_recv, q_send, q_recv,
    s_send, s_recv, y_send, y_recv, z_send, z_recv,
):
    me = lax.axis_index("ctx")
    z = me // 4
    y = (me // 2) % 2
    c = me % 2
    sibling = me + 1 - 2 * c
    y_peer = me + 2 - 4 * y

    def z_at(dz):
        return (z + dz) % ZS

    def z_peer(dz):
        return z_at(dz) * 4 + me % 4

    def block_at(dz, dy, dc):
        yy = y if dy == 0 else 1 - y
        cc = c if dc == 0 else 1 - c
        return z_at(dz) * 4 + yy * 2 + cc

    loads = [
        pltpu.make_async_copy(hidden, hidden_v, load_sem.at[0]),
        pltpu.make_async_copy(w_query, query_v, load_sem.at[1]),
        pltpu.make_async_copy(w_keyval, keyval_v, load_sem.at[2]),
        pltpu.make_async_copy(cache, cache_v, load_sem.at[3]),
        pltpu.make_async_copy(order_h, order, load_sem.at[4]),
        pltpu.make_async_copy(count_h, count, load_sem.at[5]),
        pltpu.make_async_copy(pos_h, pos, load_sem.at[6]),
        pltpu.make_async_copy(table_h, table, load_sem.at[7]),
    ]
    for at in (4, 0, 5, 6, 7, 3, 1, 2):
        loads[at].start()

    barrier = pltpu.get_barrier_semaphore()
    peers = [sibling, y_peer] + [z_peer(dz) for dz in (1, 2, 3)]
    for peer in peers:
        pl.semaphore_signal(barrier, inc=1, device_id={"ctx": peer}, device_id_type=MESH)

    loads[4].wait()
    row = lax.broadcasted_iota(jnp.int32, (16, 16), 0)
    column = lax.broadcasted_iota(jnp.int32, (16, 16), 1)
    chosen = jnp.zeros((16, 16), jnp.int32)
    for slot in range(KMAX):
        chosen = jnp.where(row % 4 == slot, order[me, slot], chosen)
    loads[0].wait()
    picked = jnp.zeros((16, WIDE), jnp.float32)
    for g in range(GROUPS):
        onehot = jnp.where((chosen == column) & (row // 4 == g), 1.0, 0.0).astype(jnp.bfloat16)
        picked += contract(onehot, hidden_v[:, g * WIDE : (g + 1) * WIDE], (1, 0))
    slots[me] = picked.astype(jnp.bfloat16)
    pl.semaphore_wait(barrier, len(peers))

    def relay(buf, send_sem, recv_sem):
        sent = []

        def send(at, receiver_at, peer):
            copy = pltpu.make_async_remote_copy(
                src_ref=buf.at[block_at(*at)],
                dst_ref=buf.at[block_at(*at)],
                send_sem=send_sem.at[len(sent)],
                recv_sem=recv_sem.at[receiver_at],
                device_id={"ctx": peer},
                device_id_type=MESH,
            )
            copy.start()
            sent.append(copy)

        def arrived(dz, dy, dc):
            pltpu.make_async_remote_copy(
                src_ref=buf.at[block_at(dz, dy, dc)],
                dst_ref=buf.at[block_at(dz, dy, dc)],
                send_sem=send_sem.at[0],
                recv_sem=recv_sem.at[dz * 4 + dy * 2 + dc],
                device_id={"ctx": sibling},
                device_id_type=MESH,
            ).wait_recv()

        def pass_on(dz, dy):
            arrived(dz, dy, 0)
            if dy == 0:
                send((dz, 0, 0), dz * 4 + 2, y_peer)
            send((dz, dy, 0), dz * 4 + dy * 2 + 1, sibling)

        for dz in (2, 1, 3):
            send((0, 0, 0), (ZS - dz) * 4, z_peer(dz))
        send((0, 0, 0), 2, y_peer)
        send((0, 0, 0), 1, sibling)
        return sent, arrived, pass_on

    def tables():
        lane = lax.broadcasted_iota(jnp.int32, (1, 256), 1)
        source = lane // 16
        local = lane % 4
        first = jnp.zeros((1, 256), jnp.int32)
        kept = jnp.zeros((1, 256), jnp.int32)
        place = jnp.zeros((1, 256), jnp.int32)
        begin = jnp.int32(0)
        for s in range(SHARDS):
            first = jnp.where(source == s, begin, first)
            kept = jnp.where(source == s, count[s], kept)
            begin = begin + count[s]
            for slot in range(KMAX):
                place = jnp.where(
                    (source == s) & (local == slot), pos[s * 16 + order[s, slot]], place
                )
        target = jnp.where(local < kept, first + local, -1)
        listed = lax.broadcasted_iota(jnp.int32, (KEEP, 256), 0) == target
        group = (lane // 4) % 4
        picks = [
            jnp.where(listed & (group == g), 1.0, 0.0).astype(jnp.bfloat16) for g in range(GROUPS)
        ]
        mine = jnp.where(listed & (group == 0), 1.0, 0.0)
        upper = jnp.sum(mine * (place >> 10).astype(jnp.float32), axis=1, keepdims=True)
        lower = jnp.sum(mine * (place & 1023).astype(jnp.float32), axis=1, keepdims=True)
        angle = lower * table[0:1, :] + upper * table[1:2, :]
        return picks, upper * 1024.0 + lower, jnp.cos(angle), jnp.sin(angle) * table[2:3, :]

    def transpose(g):
        at = (KVH + g) * HD
        values_t[g] = cache_v[:, at : at + HD].T

    row_sent, row_arrived, row_pass = relay(slots, row_send, row_recv)
    for at in (5, 6, 7):
        loads[at].wait()
    picks, places, cosine, sine = tables()
    loads[3].wait()
    filler = 0
    for dz, dy in ((0, 1), (1, 0), (3, 0), (2, 0), (1, 1), (3, 1), (2, 1)):
        row_pass(dz, dy)
        transpose(filler)
        filler += 1
    transpose(filler)
    for dy in (0, 1):
        for dz in (0, 1, 3, 2):
            row_arrived(dz, dy, 1)
    loads[1].wait()
    loads[2].wait()
    query = jnp.zeros((KEEP, 4 * HD), jnp.float32)
    keyval = jnp.zeros((KEEP, HD), jnp.float32)
    for g in range(GROUPS):
        rows = contract(picks[g], slots[...].reshape(256, WIDE), (1, 0)).astype(jnp.bfloat16)
        query += contract(rows, query_v[g * WIDE : (g + 1) * WIDE, :], (1, 0))
        keyval += contract(rows, keyval_v[g * WIDE : (g + 1) * WIDE, :], (1, 0))

    def turn(part):
        return part * cosine + pltpu.roll(part, HD // 2, 1) * sine

    for h in range(4):
        qbuf[me, h * KEEP : (h + 1) * KEEP, :] = turn(query[:, h * HD : (h + 1) * HD]).astype(
            jnp.bfloat16
        )
    plain = keyval.astype(jnp.bfloat16).astype(jnp.float32)
    qbuf[me, QROWS:, :] = jnp.where(me < KVH, turn(plain), plain).astype(jnp.bfloat16)

    q_sent, q_arrived, q_pass = relay(qbuf, q_send, q_recv)

    def attend(g):
        keys = cache_v[:, pl.ds(pl.multiple_of(g * HD, HD), HD)]
        both = jnp.concatenate(
            [qbuf[2 * g + 1 - c, :QROWS, :], qbuf[2 * g + c, :QROWS, :]], axis=0
        )
        scores = contract(keys, both, (1, 1))
        top = jnp.max(scores, axis=0, keepdims=True)
        weights = jnp.exp2((scores - top) * EXP2_SCALE)
        total = jnp.sum(weights, axis=0, keepdims=True)
        numer = contract(values_t[g], weights.astype(jnp.bfloat16), (1, 0))
        partial = numer * (1.0 / total)
        lse = top * EXP2_SCALE + jnp.log2(total)
        pack(send_s, g, partial[:, :QROWS], lse[:, :QROWS])
        own[g] = partial[:, QROWS:]
        own_lse[g] = jnp.broadcast_to(lse[:, QROWS:], (8, QROWS))

    def move(src, dst, index_from, index_to, ssem, rsem, peer):
        return pltpu.make_async_remote_copy(
            src_ref=src.at[index_from],
            dst_ref=dst.at[index_to],
            send_sem=ssem,
            recv_sem=rsem,
            device_id={"ctx": peer},
            device_id_type=MESH,
        )

    def to_sibling(dz, dy):
        g = z_at(dz) * 2 + (y if dy == 0 else 1 - y)
        at = dz * 2 + dy
        return move(send_s, recv_s, g, g, s_send.at[at], s_recv.at[at], sibling)

    def to_y(dz):
        return move(send_y, recv_y, dz, dz, y_send.at[dz], y_recv.at[dz], y_peer)

    def to_z(dz):
        return move(send_z, recv_z, dz, ZS - dz, z_send.at[dz], z_recv.at[ZS - dz], z_peer(dz))

    def mine_and_sibling(dz, dy):
        g = z_at(dz) * 2 + (y if dy == 0 else 1 - y)
        to_sibling(dz, dy).wait_recv()
        return [(own[g], own_lse[g, 0:1, :]), unpack(recv_s, g)]

    turns = [(0, 1), (1, 1), (1, 0), (3, 1), (3, 0), (2, 1), (2, 0), (0, 0)]
    passes = {0: ((0, 1), (1, 0), (3, 0)), 1: ((2, 0), (1, 1), (3, 1)), 2: ((2, 1),)}

    def follow(dz, dy):
        if dy == 1:
            pack(send_y, dz, *merge(mine_and_sibling(dz, 1)))
            to_y(dz).start()
            return None
        pieces = mine_and_sibling(dz, 0)
        to_y(dz).wait_recv()
        pieces.append(unpack(recv_y, dz))
        if dz == 0:
            return merge(pieces)
        pack(send_z, dz, *merge(pieces))
        to_z(dz).start()
        return None

    lag = 1
    local = None
    for step in range(len(turns) + lag):
        if step < len(turns):
            dz, dy = turns[step]
            for link in passes.get(step, ()):
                q_pass(*link)
            q_arrived(dz, dy, 1)
            attend(z_at(dz) * 2 + (y if dy == 0 else 1 - y))
            to_sibling(dz, dy).start()
        if step == len(turns) - 1:
            new_keys = qbuf[me // 2, QROWS:, :]
            new_values = qbuf[KVH + me // 2, QROWS:, :]
            spot = lax.broadcasted_iota(jnp.int32, (KEEP, QROWS), 0)
            lane = lax.broadcasted_iota(jnp.int32, (KEEP, QROWS), 1)
            asker = jnp.sum(jnp.where(lane % KEEP == spot, places, 0.0), axis=0, keepdims=True)
            scores = contract(new_keys, qbuf[me, :QROWS, :], (1, 1))
            seen = places <= asker
            scores = jnp.where(seen, scores, -1e30)
            top = jnp.max(scores, axis=0, keepdims=True)
            weights = jnp.where(seen, jnp.exp2((scores - top) * EXP2_SCALE), 0.0)
            total = jnp.sum(weights, axis=0, keepdims=True)
            numer = contract(new_values, weights.astype(jnp.bfloat16), (0, 0))
            fresh = (numer * (1.0 / total), top * EXP2_SCALE + jnp.log2(total))
        if step >= lag:
            local = follow(*turns[step - lag])

    pieces = [local, fresh]
    for dz in (1, 3, 2):
        pltpu.make_async_remote_copy(
            src_ref=send_z.at[dz],
            dst_ref=recv_z.at[dz],
            send_sem=z_send.at[dz],
            recv_sem=z_recv.at[dz],
            device_id={"ctx": z_peer(dz)},
            device_id_type=MESH,
        ).wait_recv()
        pieces.append(unpack(recv_z, dz))
    mixed, _ = merge(pieces)
    final = mixed.T
    for h in range(4):
        out[:, h * HD : (h + 1) * HD] = final[h * KEEP : (h + 1) * KEEP, :].astype(jnp.bfloat16)

    for copy in row_sent + q_sent:
        copy.wait_send()
    for dz, dy in turns:
        to_sibling(dz, dy).wait_send()
    for dz in range(ZS):
        to_y(dz).wait_send()
    for dz in (1, 2, 3):
        to_z(dz).wait_send()


def kernel_body(hidden, keep_order, keep_count, positions, w_query, w_keyval, cache):
    scaled, wrapped = rope_table(HD)
    sign = jnp.asarray([-1.0] * (HD // 2) + [1.0] * (HD // 2), jnp.float32)
    table = jnp.stack(
        [jnp.concatenate([scaled, scaled]), jnp.concatenate([wrapped, wrapped]), sign]
        + [jnp.zeros((HD,), jnp.float32)] * 5
    )
    vmem = pl.BlockSpec(memory_space=pltpu.VMEM)
    hbm = pl.BlockSpec(memory_space=pltpu.HBM)
    tokens = cache.shape[0]
    bf16 = jnp.bfloat16
    dma = pltpu.SemaphoreType.DMA
    return pl.pallas_call(
        kernel,
        out_shape=jax.ShapeDtypeStruct((KEEP, 4 * HD), bf16),
        in_specs=[hbm] * 8,
        out_specs=vmem,
        scratch_shapes=[
            pltpu.SMEM(keep_order.shape, jnp.int32),
            pltpu.SMEM(keep_count.shape, jnp.int32),
            pltpu.SMEM(positions.shape, jnp.int32),
            pltpu.VMEM(table.shape, jnp.float32),
            pltpu.VMEM(hidden.shape, bf16),
            pltpu.VMEM(w_query.shape, bf16),
            pltpu.VMEM(w_keyval.shape, bf16),
            pltpu.VMEM(cache.shape, bf16),
            pltpu.VMEM((SHARDS, 16, WIDE), bf16),
            pltpu.VMEM((SHARDS, QROWS + KEEP, HD), bf16),
            pltpu.VMEM((KVH, HD, tokens), bf16),
            pltpu.VMEM((KVH, HD, QROWS), jnp.float32),
            pltpu.VMEM((KVH, 8, QROWS), jnp.float32),
            pltpu.VMEM((KVH, MSG, QROWS), bf16),
            pltpu.VMEM((KVH, MSG, QROWS), bf16),
            pltpu.VMEM((ZS, MSG, QROWS), bf16),
            pltpu.VMEM((ZS, MSG, QROWS), bf16),
            pltpu.VMEM((ZS, MSG, QROWS), bf16),
            pltpu.VMEM((ZS, MSG, QROWS), bf16),
            dma((8,)),
            dma((15,)),
            dma((16,)),
            dma((15,)),
            dma((16,)),
            dma((8,)),
            dma((8,)),
            dma((4,)),
            dma((4,)),
            dma((4,)),
            dma((4,)),
        ],
        compiler_params=pltpu.CompilerParams(
            collective_id=0, has_side_effects=True, vmem_limit_bytes=64 * 1024 * 1024 - 64 * 1024
        ),
        cost_estimate=pl.CostEstimate(
            flops=1_500_000_000, bytes_accessed=15_000_000, transcendentals=2_100_000
        ),
    )(keep_order, keep_count, positions, table, hidden, w_query, w_keyval, cache)


def solution(mesh):
    use = kernel_body if mesh.shape["ctx"] == 16 else body
    return jax.shard_map(
        use,
        mesh=mesh,
        in_specs=(
            P(("req", "ctx"), None),
            P("req", None),
            P("req"),
            P("req"),
            P(None, "ctx"),
            P(None, "ctx"),
            P(("req", "ctx"), None),
        ),
        out_specs=P("req", "ctx"),
        check_vma=False,
    )
```

```python
import functools
import math

import jax
import jax.numpy as jnp
from jax import lax
from jax.experimental import pallas as pl
from jax.experimental.pallas import tpu as pltpu
from jax.sharding import PartitionSpec as P

H = 64
KVH = 8
HD = 128
KEEP_DEV = 2
KMAX = 4


def rope_table(head_size):
    half = head_size // 2
    period = 2.0 * math.pi
    scaled_list = []
    wrapped_list = []
    for column in range(half):
        inverse = 500000.0 ** (-2.0 * column / head_size)
        wavelen = 2.0 * math.pi / inverse
        if wavelen > 8192.0:
            scaled_rate = inverse / 8.0
        elif wavelen < 2048.0:
            scaled_rate = inverse
        else:
            smooth = (8192.0 / wavelen - 1.0) / 3.0
            scaled_rate = (1.0 - smooth) * inverse / 8.0 + smooth * inverse
        scaled_list.append(scaled_rate)
        step_angle = 1024.0 * scaled_rate
        wrapped_list.append(step_angle - period * (step_angle // period))
    return (jnp.asarray(scaled_list, jnp.float32), jnp.asarray(wrapped_list, jnp.float32))


def rotate(values, places):
    scaled, wrapped = rope_table(values.shape[-1])
    upper = (places // 1024).astype(jnp.float32)
    lower = (places % 1024).astype(jnp.float32)
    angle = lower[:, None] * scaled[None, :] + upper[:, None] * wrapped[None, :]
    cosine = jnp.cos(angle)[:, None, :]
    sine = jnp.sin(angle)[:, None, :]
    half = values.shape[-1] // 2
    first = values[..., :half]
    second = values[..., half:]
    return jnp.concatenate(
        [first * cosine - second * sine, second * cosine + first * sine], axis=-1
    )


def kept_sources(keep_count, kept_total, shards):
    ends = jnp.cumsum(keep_count)
    starts = ends - keep_count
    slots = jnp.arange(kept_total, dtype=jnp.int32)
    owner = jnp.sum((ends[None, :] <= slots[:, None]).astype(jnp.int32), axis=1)
    ids = jnp.arange(shards, dtype=jnp.int32)
    first = jnp.sum(jnp.where(ids[None, :] == owner[:, None], starts[None, :], 0), axis=1)
    return (owner, slots - first)


def body(hidden, keep_order, keep_count, positions, w_query, w_keyval, cache):
    shards = lax.axis_size("ctx")
    me = lax.axis_index("ctx")
    span_rows = hidden.shape[0]
    kept_total = KEEP_DEV * shards
    block = KEEP_DEV
    cache_rows = cache.shape[0]
    heads_here = H // shards
    order_here = lax.dynamic_slice_in_dim(keep_order, me, 1, 0)[0, :KMAX]
    slot_rows = hidden[order_here]
    rows_all = lax.all_gather(slot_rows, "ctx", axis=0, tiled=True)
    owner, local = kept_sources(keep_count, kept_total, shards)
    rows = rows_all[owner * KMAX + local]
    places = positions[owner * span_rows + keep_order[owner, local]]
    query = jnp.dot(rows, w_query, preferred_element_type=jnp.float32).reshape(
        kept_total, heads_here, HD
    )
    query = rotate(query, places).astype(jnp.bfloat16).reshape(kept_total, heads_here * HD)
    key_part = jnp.dot(rows, w_keyval, preferred_element_type=jnp.float32).astype(jnp.bfloat16)
    own_keyval = lax.all_to_all(key_part, "ctx", split_axis=0, concat_axis=1, tiled=True)
    own_places = lax.dynamic_slice_in_dim(places, me * block, block, 0)
    new_keys = rotate(
        own_keyval[:, : KVH * HD].astype(jnp.float32).reshape(block, KVH, HD), own_places
    )
    new_keys = new_keys.astype(jnp.bfloat16).reshape(block, KVH * HD)
    keys = jnp.concatenate([cache[:, : KVH * HD], new_keys], axis=0)
    values = jnp.concatenate([cache[:, KVH * HD :], own_keyval[:, KVH * HD :]], axis=0)
    queries = lax.all_gather(query, "ctx", axis=1, tiled=True)
    visible = jnp.concatenate(
        [jnp.ones((kept_total, cache_rows), bool), own_places[None, :] <= places[:, None]], axis=1
    )
    group = H // KVH
    scale = 1.0 / math.sqrt(HD)
    numer_list = []
    top_list = []
    total_list = []
    for index in range(KVH):
        q_group = queries[:, index * group * HD : (index + 1) * group * HD].reshape(
            kept_total, group, HD
        )
        k_group = keys[:, index * HD : (index + 1) * HD]
        v_group = values[:, index * HD : (index + 1) * HD]
        scores = (
            jnp.einsum("qhd,kd->qhk", q_group, k_group, preferred_element_type=jnp.float32) * scale
        )
        scores = jnp.where(visible[:, None, :], scores, -1e30)
        top = jnp.max(scores, axis=2)
        weights = jnp.exp(scores - top[..., None])
        total_list.append(jnp.sum(weights, axis=2))
        top_list.append(top)
        numer = jnp.einsum(
            "qhk,kd->qhd", weights.astype(jnp.bfloat16), v_group, preferred_element_type=jnp.float32
        )
        numer_list.append(numer.reshape(kept_total, group * HD))
    numer = jnp.concatenate(numer_list, axis=1)
    top = jnp.concatenate(top_list, axis=1)
    total = jnp.concatenate(total_list, axis=1)
    best = lax.pmax(top.astype(jnp.bfloat16), "ctx").astype(top.dtype)
    factor = jnp.exp(top - best)
    scaled_numer = (numer.reshape(kept_total, H, HD) * factor[..., None]).reshape(
        kept_total, H * HD
    )
    result, denom = (
        lax.psum_scatter(scaled_numer, "ctx", scatter_dimension=1, tiled=True),
        lax.psum_scatter(total * factor, "ctx", scatter_dimension=1, tiled=True),
    )
    result = result.reshape(kept_total, heads_here, HD)
    return (result / denom[..., None]).reshape(kept_total, heads_here * HD).astype(jnp.bfloat16)


MESH = pl.DeviceIdType.MESH
ZS = 4
SHARDS = 16
KEEP = 32
GROUPS = 4
WIDE = 2048
QROWS = 128
SCHEDULE = (
    (0, 1, 0),
    (1, 0, 0),
    (3, 0, 0),
    (1, 1, 0),
    (3, 1, 0),
    (0, 1, 1),
    (2, 1, 0),
    (1, 1, 1),
    (2, 0, 0),
    (3, 1, 1),
    (0, 0, 0),
    (2, 1, 1),
    (1, 0, 1),
    (3, 0, 1),
    (2, 0, 1),
    (0, 0, 1),
)
EXP2_SCALE = math.log2(math.e) / math.sqrt(HD)
MSG = QROWS + 16


def pack(ref, index, partial, lse):
    ref[index, :QROWS, :] = partial.astype(jnp.bfloat16)
    high = lse.astype(jnp.bfloat16).astype(jnp.float32)
    middle = (lse - high).astype(jnp.bfloat16).astype(jnp.float32)
    low = lse - high - middle
    row = lax.broadcasted_iota(jnp.int32, (16, QROWS), 0)
    stats = jnp.where(row == 0, high, jnp.where(row == 1, middle, jnp.where(row == 2, low, 0.0)))
    ref[index, QROWS:, :] = stats.astype(jnp.bfloat16)


def unpack(ref, index):
    stats = ref[index, QROWS:, :].astype(jnp.float32)
    return ref[index, :QROWS, :].astype(jnp.float32), jnp.sum(stats, axis=0, keepdims=True)


def merge(pieces):
    best = functools.reduce(jnp.maximum, [lse for _, lse in pieces])
    factors = [jnp.exp2(lse - best) for _, lse in pieces]
    total = sum(factors)
    inverse = 1.0 / total
    mixed = sum(partial * (factor * inverse) for (partial, _), factor in zip(pieces, factors))
    return mixed, best + jnp.log2(total)


def contract(a, b, dims):
    return lax.dot_general(a, b, ((dims[:1], dims[1:]), ((), ())), preferred_element_type=jnp.float32)


def kernel(
    order_h, count_h, pos_h, table_h, hidden, w_query, w_keyval, cache, out,
    order, count, pos, table, hidden_v, query_v, keyval_v, cache_v, slots, qbuf, values_t,
    own, own_lse, send_s, recv_s, send_y, recv_y, send_z, recv_z,
    load_sem, row_send, row_recv, q_send, q_recv,
    s_send, s_recv, y_send, y_recv, z_send, z_recv,
):
    me = lax.axis_index("ctx")
    z = me // 4
    y = (me // 2) % 2
    c = me % 2
    sibling = me + 1 - 2 * c
    y_peer = me + 2 - 4 * y

    def z_at(dz):
        return (z + dz) % ZS

    def z_peer(dz):
        return z_at(dz) * 4 + me % 4

    def block_at(dz, dy, dc):
        yy = y if dy == 0 else 1 - y
        cc = c if dc == 0 else 1 - c
        return z_at(dz) * 4 + yy * 2 + cc

    loads = [
        pltpu.make_async_copy(hidden, hidden_v, load_sem.at[0]),
        pltpu.make_async_copy(w_query, query_v, load_sem.at[1]),
        pltpu.make_async_copy(w_keyval, keyval_v, load_sem.at[2]),
        pltpu.make_async_copy(cache, cache_v, load_sem.at[3]),
        pltpu.make_async_copy(order_h, order, load_sem.at[4]),
        pltpu.make_async_copy(count_h, count, load_sem.at[5]),
        pltpu.make_async_copy(pos_h, pos, load_sem.at[6]),
        pltpu.make_async_copy(table_h, table, load_sem.at[7]),
    ]
    for at in (4, 0, 5, 6, 7, 3, 1, 2):
        loads[at].start()

    barrier = pltpu.get_barrier_semaphore()
    peers = [sibling, y_peer] + [z_peer(dz) for dz in (1, 2, 3)]
    for peer in peers:
        pl.semaphore_signal(barrier, inc=1, device_id={"ctx": peer}, device_id_type=MESH)

    loads[4].wait()
    row = lax.broadcasted_iota(jnp.int32, (16, 16), 0)
    column = lax.broadcasted_iota(jnp.int32, (16, 16), 1)
    chosen = jnp.zeros((16, 16), jnp.int32)
    for slot in range(KMAX):
        chosen = jnp.where(row % 4 == slot, order[me, slot], chosen)
    loads[0].wait()
    picked = jnp.zeros((16, WIDE), jnp.float32)
    for g in range(GROUPS):
        onehot = jnp.where((chosen == column) & (row // 4 == g), 1.0, 0.0).astype(jnp.bfloat16)
        picked += contract(onehot, hidden_v[:, g * WIDE : (g + 1) * WIDE], (1, 0))
    slots[me] = picked.astype(jnp.bfloat16)
    pl.semaphore_wait(barrier, len(peers))

    def relay(buf, send_sem, recv_sem):
        sent = []

        def send(at, receiver_at, peer):
            copy = pltpu.make_async_remote_copy(
                src_ref=buf.at[block_at(*at)],
                dst_ref=buf.at[block_at(*at)],
                send_sem=send_sem.at[len(sent)],
                recv_sem=recv_sem.at[receiver_at],
                device_id={"ctx": peer},
                device_id_type=MESH,
            )
            copy.start()
            sent.append(copy)

        def arrived(dz, dy, dc):
            pltpu.make_async_remote_copy(
                src_ref=buf.at[block_at(dz, dy, dc)],
                dst_ref=buf.at[block_at(dz, dy, dc)],
                send_sem=send_sem.at[0],
                recv_sem=recv_sem.at[dz * 4 + dy * 2 + dc],
                device_id={"ctx": sibling},
                device_id_type=MESH,
            ).wait_recv()

        def pass_on(dz, dy):
            arrived(dz, dy, 0)
            if dy == 0:
                send((dz, 0, 0), dz * 4 + 2, y_peer)
            send((dz, dy, 0), dz * 4 + dy * 2 + 1, sibling)

        for dz in (2, 1, 3):
            send((0, 0, 0), (ZS - dz) * 4, z_peer(dz))
        send((0, 0, 0), 2, y_peer)
        send((0, 0, 0), 1, sibling)
        return sent, arrived, pass_on

    def tables():
        lane = lax.broadcasted_iota(jnp.int32, (1, 256), 1)
        source = lane // 16
        local = lane % 4
        first = jnp.zeros((1, 256), jnp.int32)
        kept = jnp.zeros((1, 256), jnp.int32)
        place = jnp.zeros((1, 256), jnp.int32)
        begin = jnp.int32(0)
        for s in range(SHARDS):
            first = jnp.where(source == s, begin, first)
            kept = jnp.where(source == s, count[s], kept)
            begin = begin + count[s]
            for slot in range(KMAX):
                place = jnp.where(
                    (source == s) & (local == slot), pos[s * 16 + order[s, slot]], place
                )
        target = jnp.where(local < kept, first + local, -1)
        listed = lax.broadcasted_iota(jnp.int32, (KEEP, 256), 0) == target
        group = (lane // 4) % 4
        picks = [
            jnp.where(listed & (group == g), 1.0, 0.0).astype(jnp.bfloat16) for g in range(GROUPS)
        ]
        mine = jnp.where(listed & (group == 0), 1.0, 0.0)
        upper = jnp.sum(mine * (place >> 10).astype(jnp.float32), axis=1, keepdims=True)
        lower = jnp.sum(mine * (place & 1023).astype(jnp.float32), axis=1, keepdims=True)
        angle = lower * table[0:1, :] + upper * table[1:2, :]
        return picks, upper * 1024.0 + lower, jnp.cos(angle), jnp.sin(angle) * table[2:3, :]

    def transpose(g):
        at = (KVH + g) * HD
        values_t[g] = cache_v[:, at : at + HD].T

    row_sent, row_arrived, row_pass = relay(slots, row_send, row_recv)
    for at in (5, 6, 7):
        loads[at].wait()
    picks, places, cosine, sine = tables()
    loads[3].wait()
    filler = 0
    for dz, dy in ((0, 1), (1, 0), (3, 0), (2, 0), (1, 1), (3, 1), (2, 1)):
        row_pass(dz, dy)
        transpose(filler)
        filler += 1
    transpose(filler)
    for dy in (0, 1):
        for dz in (0, 1, 3, 2):
            row_arrived(dz, dy, 1)
    loads[1].wait()
    loads[2].wait()
    query = jnp.zeros((KEEP, 4 * HD), jnp.float32)
    keyval = jnp.zeros((KEEP, HD), jnp.float32)
    for g in range(GROUPS):
        rows = contract(picks[g], slots[...].reshape(256, WIDE), (1, 0)).astype(jnp.bfloat16)
        query += contract(rows, query_v[g * WIDE : (g + 1) * WIDE, :], (1, 0))
        keyval += contract(rows, keyval_v[g * WIDE : (g + 1) * WIDE, :], (1, 0))

    def turn(part):
        return part * cosine + pltpu.roll(part, HD // 2, 1) * sine

    for h in range(4):
        qbuf[me, h * KEEP : (h + 1) * KEEP, :] = turn(query[:, h * HD : (h + 1) * HD]).astype(
            jnp.bfloat16
        )
    plain = keyval.astype(jnp.bfloat16).astype(jnp.float32)
    qbuf[me, QROWS:, :] = jnp.where(me < KVH, turn(plain), plain).astype(jnp.bfloat16)

    q_sent, q_arrived, q_pass = relay(qbuf, q_send, q_recv)

    def attend(g):
        keys = cache_v[:, pl.ds(pl.multiple_of(g * HD, HD), HD)]
        both = jnp.concatenate(
            [qbuf[2 * g + 1 - c, :QROWS, :], qbuf[2 * g + c, :QROWS, :]], axis=0
        )
        scores = contract(keys, both, (1, 1))
        top = jnp.max(scores, axis=0, keepdims=True)
        weights = jnp.exp2((scores - top) * EXP2_SCALE)
        total = jnp.sum(weights, axis=0, keepdims=True)
        numer = contract(values_t[g], weights.astype(jnp.bfloat16), (1, 0))
        partial = numer * (1.0 / total)
        lse = top * EXP2_SCALE + jnp.log2(total)
        pack(send_s, g, partial[:, :QROWS], lse[:, :QROWS])
        own[g] = partial[:, QROWS:]
        own_lse[g] = jnp.broadcast_to(lse[:, QROWS:], (8, QROWS))

    def move(src, dst, index_from, index_to, ssem, rsem, peer):
        return pltpu.make_async_remote_copy(
            src_ref=src.at[index_from],
            dst_ref=dst.at[index_to],
            send_sem=ssem,
            recv_sem=rsem,
            device_id={"ctx": peer},
            device_id_type=MESH,
        )

    def to_sibling(dz, dy):
        g = z_at(dz) * 2 + (y if dy == 0 else 1 - y)
        at = dz * 2 + dy
        return move(send_s, recv_s, g, g, s_send.at[at], s_recv.at[at], sibling)

    def to_y(dz):
        return move(send_y, recv_y, dz, dz, y_send.at[dz], y_recv.at[dz], y_peer)

    def to_z(dz):
        return move(send_z, recv_z, dz, ZS - dz, z_send.at[dz], z_recv.at[ZS - dz], z_peer(dz))

    def mine_and_sibling(dz, dy):
        g = z_at(dz) * 2 + (y if dy == 0 else 1 - y)
        to_sibling(dz, dy).wait_recv()
        return [(own[g], own_lse[g, 0:1, :]), unpack(recv_s, g)]

    turns = [(dz, dy) for dz in range(ZS) for dy in (0, 1)]
    passes = {0: ((0, 1), (1, 0), (3, 0)), 1: ((2, 0),), 3: ((1, 1), (3, 1), (2, 1))}

    def follow(dz, dy):
        if dy == 1:
            pack(send_y, dz, *merge(mine_and_sibling(dz, 1)))
            to_y(dz).start()
            return None
        pieces = mine_and_sibling(dz, 0)
        to_y(dz).wait_recv()
        pieces.append(unpack(recv_y, dz))
        if dz == 0:
            return merge(pieces)
        pack(send_z, dz, *merge(pieces))
        to_z(dz).start()
        return None

    def fresh_keys():
        new_keys = qbuf[me // 2, QROWS:, :]
        new_values = qbuf[KVH + me // 2, QROWS:, :]
        spot = lax.broadcasted_iota(jnp.int32, (KEEP, QROWS), 0)
        lane = lax.broadcasted_iota(jnp.int32, (KEEP, QROWS), 1)
        asker = jnp.sum(jnp.where(lane % KEEP == spot, places, 0.0), axis=0, keepdims=True)
        scores = contract(new_keys, qbuf[me, :QROWS, :], (1, 1))
        seen = places <= asker
        scores = jnp.where(seen, scores, -1e30)
        top = jnp.max(scores, axis=0, keepdims=True)
        weights = jnp.where(seen, jnp.exp2((scores - top) * EXP2_SCALE), 0.0)
        total = jnp.sum(weights, axis=0, keepdims=True)
        numer = contract(new_values, weights.astype(jnp.bfloat16), (0, 0))
        fresh = (numer * (1.0 / total), top * EXP2_SCALE + jnp.log2(total))
        return fresh

    local = None
    fresh = None
    attended = 0
    for dz, dy, done in SCHEDULE:
        if done:
            local = follow(dz, dy)
            continue
        for link in passes.get(attended, ()):
            q_pass(*link)
        q_arrived(dz, dy, 1)
        attend(z_at(dz) * 2 + (y if dy == 0 else 1 - y))
        to_sibling(dz, dy).start()
        attended += 1
        if attended == KVH:
            fresh = fresh_keys()

    pieces = [local, fresh]
    for dz in (1, 3, 2):
        pltpu.make_async_remote_copy(
            src_ref=send_z.at[dz],
            dst_ref=recv_z.at[dz],
            send_sem=z_send.at[dz],
            recv_sem=z_recv.at[dz],
            device_id={"ctx": z_peer(dz)},
            device_id_type=MESH,
        ).wait_recv()
        pieces.append(unpack(recv_z, dz))
    mixed, _ = merge(pieces)
    final = mixed.T
    for h in range(4):
        out[:, h * HD : (h + 1) * HD] = final[h * KEEP : (h + 1) * KEEP, :].astype(jnp.bfloat16)

    for copy in row_sent + q_sent:
        copy.wait_send()
    for dz, dy in turns:
        to_sibling(dz, dy).wait_send()
    for dz in range(ZS):
        to_y(dz).wait_send()
    for dz in (1, 2, 3):
        to_z(dz).wait_send()


def kernel_body(hidden, keep_order, keep_count, positions, w_query, w_keyval, cache):
    scaled, wrapped = rope_table(HD)
    sign = jnp.asarray([-1.0] * (HD // 2) + [1.0] * (HD // 2), jnp.float32)
    table = jnp.stack(
        [jnp.concatenate([scaled, scaled]), jnp.concatenate([wrapped, wrapped]), sign]
        + [jnp.zeros((HD,), jnp.float32)] * 5
    )
    vmem = pl.BlockSpec(memory_space=pltpu.VMEM)
    hbm = pl.BlockSpec(memory_space=pltpu.HBM)
    tokens = cache.shape[0]
    bf16 = jnp.bfloat16
    dma = pltpu.SemaphoreType.DMA
    return pl.pallas_call(
        kernel,
        out_shape=jax.ShapeDtypeStruct((KEEP, 4 * HD), bf16),
        in_specs=[hbm] * 8,
        out_specs=vmem,
        scratch_shapes=[
            pltpu.SMEM(keep_order.shape, jnp.int32),
            pltpu.SMEM(keep_count.shape, jnp.int32),
            pltpu.SMEM(positions.shape, jnp.int32),
            pltpu.VMEM(table.shape, jnp.float32),
            pltpu.VMEM(hidden.shape, bf16),
            pltpu.VMEM(w_query.shape, bf16),
            pltpu.VMEM(w_keyval.shape, bf16),
            pltpu.VMEM(cache.shape, bf16),
            pltpu.VMEM((SHARDS, 16, WIDE), bf16),
            pltpu.VMEM((SHARDS, QROWS + KEEP, HD), bf16),
            pltpu.VMEM((KVH, HD, tokens), bf16),
            pltpu.VMEM((KVH, HD, QROWS), jnp.float32),
            pltpu.VMEM((KVH, 8, QROWS), jnp.float32),
            pltpu.VMEM((KVH, MSG, QROWS), bf16),
            pltpu.VMEM((KVH, MSG, QROWS), bf16),
            pltpu.VMEM((ZS, MSG, QROWS), bf16),
            pltpu.VMEM((ZS, MSG, QROWS), bf16),
            pltpu.VMEM((ZS, MSG, QROWS), bf16),
            pltpu.VMEM((ZS, MSG, QROWS), bf16),
            dma((8,)),
            dma((15,)),
            dma((16,)),
            dma((15,)),
            dma((16,)),
            dma((8,)),
            dma((8,)),
            dma((4,)),
            dma((4,)),
            dma((4,)),
            dma((4,)),
        ],
        compiler_params=pltpu.CompilerParams(
            collective_id=0, has_side_effects=True, vmem_limit_bytes=64 * 1024 * 1024 - 64 * 1024
        ),
        cost_estimate=pl.CostEstimate(
            flops=1_500_000_000, bytes_accessed=15_000_000, transcendentals=2_100_000
        ),
    )(keep_order, keep_count, positions, table, hidden, w_query, w_keyval, cache)


def solution(mesh):
    use = kernel_body if mesh.shape["ctx"] == 16 else body
    return jax.shard_map(
        use,
        mesh=mesh,
        in_specs=(
            P(("req", "ctx"), None),
            P("req", None),
            P("req"),
            P("req"),
            P(None, "ctx"),
            P(None, "ctx"),
            P(("req", "ctx"), None),
        ),
        out_specs=P("req", "ctx"),
        check_vma=False,
    )
```

```python
import functools
import math

import jax
import jax.numpy as jnp
from jax import lax
from jax.experimental import pallas as pl
from jax.experimental.pallas import tpu as pltpu
from jax.sharding import PartitionSpec as P

H = 64
KVH = 8
HD = 128
KEEP_DEV = 2
KMAX = 4


def rope_table(head_size):
    half = head_size // 2
    period = 2.0 * math.pi
    scaled_list = []
    wrapped_list = []
    for column in range(half):
        inverse = 500000.0 ** (-2.0 * column / head_size)
        wavelen = 2.0 * math.pi / inverse
        if wavelen > 8192.0:
            scaled_rate = inverse / 8.0
        elif wavelen < 2048.0:
            scaled_rate = inverse
        else:
            smooth = (8192.0 / wavelen - 1.0) / 3.0
            scaled_rate = (1.0 - smooth) * inverse / 8.0 + smooth * inverse
        scaled_list.append(scaled_rate)
        step_angle = 1024.0 * scaled_rate
        wrapped_list.append(step_angle - period * (step_angle // period))
    return (jnp.asarray(scaled_list, jnp.float32), jnp.asarray(wrapped_list, jnp.float32))


def rotate(values, places):
    scaled, wrapped = rope_table(values.shape[-1])
    upper = (places // 1024).astype(jnp.float32)
    lower = (places % 1024).astype(jnp.float32)
    angle = lower[:, None] * scaled[None, :] + upper[:, None] * wrapped[None, :]
    cosine = jnp.cos(angle)[:, None, :]
    sine = jnp.sin(angle)[:, None, :]
    half = values.shape[-1] // 2
    first = values[..., :half]
    second = values[..., half:]
    return jnp.concatenate(
        [first * cosine - second * sine, second * cosine + first * sine], axis=-1
    )


def kept_sources(keep_count, kept_total, shards):
    ends = jnp.cumsum(keep_count)
    starts = ends - keep_count
    slots = jnp.arange(kept_total, dtype=jnp.int32)
    owner = jnp.sum((ends[None, :] <= slots[:, None]).astype(jnp.int32), axis=1)
    ids = jnp.arange(shards, dtype=jnp.int32)
    first = jnp.sum(jnp.where(ids[None, :] == owner[:, None], starts[None, :], 0), axis=1)
    return (owner, slots - first)


def body(hidden, keep_order, keep_count, positions, w_query, w_keyval, cache):
    shards = lax.axis_size("ctx")
    me = lax.axis_index("ctx")
    span_rows = hidden.shape[0]
    kept_total = KEEP_DEV * shards
    block = KEEP_DEV
    cache_rows = cache.shape[0]
    heads_here = H // shards
    order_here = lax.dynamic_slice_in_dim(keep_order, me, 1, 0)[0, :KMAX]
    slot_rows = hidden[order_here]
    rows_all = lax.all_gather(slot_rows, "ctx", axis=0, tiled=True)
    owner, local = kept_sources(keep_count, kept_total, shards)
    rows = rows_all[owner * KMAX + local]
    places = positions[owner * span_rows + keep_order[owner, local]]
    query = jnp.dot(rows, w_query, preferred_element_type=jnp.float32).reshape(
        kept_total, heads_here, HD
    )
    query = rotate(query, places).astype(jnp.bfloat16).reshape(kept_total, heads_here * HD)
    key_part = jnp.dot(rows, w_keyval, preferred_element_type=jnp.float32).astype(jnp.bfloat16)
    own_keyval = lax.all_to_all(key_part, "ctx", split_axis=0, concat_axis=1, tiled=True)
    own_places = lax.dynamic_slice_in_dim(places, me * block, block, 0)
    new_keys = rotate(
        own_keyval[:, : KVH * HD].astype(jnp.float32).reshape(block, KVH, HD), own_places
    )
    new_keys = new_keys.astype(jnp.bfloat16).reshape(block, KVH * HD)
    keys = jnp.concatenate([cache[:, : KVH * HD], new_keys], axis=0)
    values = jnp.concatenate([cache[:, KVH * HD :], own_keyval[:, KVH * HD :]], axis=0)
    queries = lax.all_gather(query, "ctx", axis=1, tiled=True)
    visible = jnp.concatenate(
        [jnp.ones((kept_total, cache_rows), bool), own_places[None, :] <= places[:, None]], axis=1
    )
    group = H // KVH
    scale = 1.0 / math.sqrt(HD)
    numer_list = []
    top_list = []
    total_list = []
    for index in range(KVH):
        q_group = queries[:, index * group * HD : (index + 1) * group * HD].reshape(
            kept_total, group, HD
        )
        k_group = keys[:, index * HD : (index + 1) * HD]
        v_group = values[:, index * HD : (index + 1) * HD]
        scores = (
            jnp.einsum("qhd,kd->qhk", q_group, k_group, preferred_element_type=jnp.float32) * scale
        )
        scores = jnp.where(visible[:, None, :], scores, -1e30)
        top = jnp.max(scores, axis=2)
        weights = jnp.exp(scores - top[..., None])
        total_list.append(jnp.sum(weights, axis=2))
        top_list.append(top)
        numer = jnp.einsum(
            "qhk,kd->qhd", weights.astype(jnp.bfloat16), v_group, preferred_element_type=jnp.float32
        )
        numer_list.append(numer.reshape(kept_total, group * HD))
    numer = jnp.concatenate(numer_list, axis=1)
    top = jnp.concatenate(top_list, axis=1)
    total = jnp.concatenate(total_list, axis=1)
    best = lax.pmax(top.astype(jnp.bfloat16), "ctx").astype(top.dtype)
    factor = jnp.exp(top - best)
    scaled_numer = (numer.reshape(kept_total, H, HD) * factor[..., None]).reshape(
        kept_total, H * HD
    )
    result, denom = (
        lax.psum_scatter(scaled_numer, "ctx", scatter_dimension=1, tiled=True),
        lax.psum_scatter(total * factor, "ctx", scatter_dimension=1, tiled=True),
    )
    result = result.reshape(kept_total, heads_here, HD)
    return (result / denom[..., None]).reshape(kept_total, heads_here * HD).astype(jnp.bfloat16)


MESH = pl.DeviceIdType.MESH
ZS = 4
SHARDS = 16
KEEP = 32
GROUPS = 4
WIDE = 2048
QROWS = 128
SCHEDULE = (
    (0, 1, 0),
    (1, 0, 0),
    (3, 0, 0),
    (1, 1, 0),
    (3, 1, 0),
    (0, 1, 1),
    (2, 1, 0),
    (1, 1, 1),
    (2, 0, 0),
    (3, 1, 1),
    (0, 0, 0),
    (2, 1, 1),
    (1, 0, 1),
    (3, 0, 1),
    (2, 0, 1),
    (0, 0, 1),
)
EXP2_SCALE = math.log2(math.e) / math.sqrt(HD)
MSG = QROWS + 16


def pack(ref, index, partial, lse):
    ref[index, :QROWS, :] = partial.astype(jnp.bfloat16)
    high = lse.astype(jnp.bfloat16).astype(jnp.float32)
    middle = (lse - high).astype(jnp.bfloat16).astype(jnp.float32)
    low = lse - high - middle
    row = lax.broadcasted_iota(jnp.int32, (16, QROWS), 0)
    stats = jnp.where(row == 0, high, jnp.where(row == 1, middle, jnp.where(row == 2, low, 0.0)))
    ref[index, QROWS:, :] = stats.astype(jnp.bfloat16)


def unpack(ref, index):
    stats = ref[index, QROWS:, :].astype(jnp.float32)
    return ref[index, :QROWS, :].astype(jnp.float32), jnp.sum(stats, axis=0, keepdims=True)


def merge(pieces):
    best = functools.reduce(jnp.maximum, [lse for _, lse in pieces])
    factors = [jnp.exp2(lse - best) for _, lse in pieces]
    total = sum(factors)
    inverse = 1.0 / total
    mixed = sum(partial * (factor * inverse) for (partial, _), factor in zip(pieces, factors))
    return mixed, best + jnp.log2(total)


def contract(a, b, dims):
    return lax.dot_general(a, b, ((dims[:1], dims[1:]), ((), ())), preferred_element_type=jnp.float32)


def kernel(
    order_h, count_h, pos_h, table_h, hidden, w_query, w_keyval, cache, out,
    order, count, pos, table, hidden_v, query_v, keyval_v, cache_v, slots, qbuf, values_t,
    own, own_lse, send_s, recv_s, send_y, recv_y, send_z, recv_z,
    load_sem, row_send, row_recv, q_send, q_recv,
    s_send, s_recv, y_send, y_recv, z_send, z_recv,
):
    me = lax.axis_index("ctx")
    z = me // 4
    y = (me // 2) % 2
    c = me % 2
    sibling = me + 1 - 2 * c
    y_peer = me + 2 - 4 * y

    def z_at(dz):
        return (z + dz) % ZS

    def z_peer(dz):
        return z_at(dz) * 4 + me % 4

    def block_at(dz, dy, dc):
        yy = y if dy == 0 else 1 - y
        cc = c if dc == 0 else 1 - c
        return z_at(dz) * 4 + yy * 2 + cc

    loads = [
        pltpu.make_async_copy(hidden, hidden_v, load_sem.at[0]),
        pltpu.make_async_copy(w_query, query_v, load_sem.at[1]),
        pltpu.make_async_copy(w_keyval, keyval_v, load_sem.at[2]),
        pltpu.make_async_copy(cache, cache_v, load_sem.at[3]),
        pltpu.make_async_copy(order_h, order, load_sem.at[4]),
        pltpu.make_async_copy(count_h, count, load_sem.at[5]),
        pltpu.make_async_copy(pos_h, pos, load_sem.at[6]),
        pltpu.make_async_copy(table_h, table, load_sem.at[7]),
    ]
    for at in (4, 0, 5, 6, 7, 3, 1, 2):
        loads[at].start()

    barrier = pltpu.get_barrier_semaphore()
    peers = [sibling, y_peer] + [z_peer(dz) for dz in (1, 2, 3)]
    for peer in peers:
        pl.semaphore_signal(barrier, inc=1, device_id={"ctx": peer}, device_id_type=MESH)

    loads[4].wait()
    row = lax.broadcasted_iota(jnp.int32, (16, 16), 0)
    column = lax.broadcasted_iota(jnp.int32, (16, 16), 1)
    chosen = jnp.zeros((16, 16), jnp.int32)
    for slot in range(KMAX):
        chosen = jnp.where(row % 4 == slot, order[me, slot], chosen)
    loads[0].wait()
    picked = jnp.zeros((16, WIDE), jnp.float32)
    for g in range(GROUPS):
        onehot = jnp.where((chosen == column) & (row // 4 == g), 1.0, 0.0).astype(jnp.bfloat16)
        picked += contract(onehot, hidden_v[:, g * WIDE : (g + 1) * WIDE], (1, 0))
    slots[me] = picked.astype(jnp.bfloat16)
    pl.semaphore_wait(barrier, len(peers))

    def relay(buf, send_sem, recv_sem):
        sent = []

        def send(at, receiver_at, peer):
            copy = pltpu.make_async_remote_copy(
                src_ref=buf.at[block_at(*at)],
                dst_ref=buf.at[block_at(*at)],
                send_sem=send_sem.at[len(sent)],
                recv_sem=recv_sem.at[receiver_at],
                device_id={"ctx": peer},
                device_id_type=MESH,
            )
            copy.start()
            sent.append(copy)

        def arrived(dz, dy, dc):
            pltpu.make_async_remote_copy(
                src_ref=buf.at[block_at(dz, dy, dc)],
                dst_ref=buf.at[block_at(dz, dy, dc)],
                send_sem=send_sem.at[0],
                recv_sem=recv_sem.at[dz * 4 + dy * 2 + dc],
                device_id={"ctx": sibling},
                device_id_type=MESH,
            ).wait_recv()

        def pass_on(dz, dy):
            arrived(dz, dy, 0)
            if dy == 0:
                send((dz, 0, 0), dz * 4 + 2, y_peer)
            send((dz, dy, 0), dz * 4 + dy * 2 + 1, sibling)

        send((0, 0, 0), 2, y_peer)
        send((0, 0, 0), 1, sibling)
        for dz in (1, 3, 2):
            send((0, 0, 0), (ZS - dz) * 4, z_peer(dz))
        return sent, arrived, pass_on

    def tables():
        lane = lax.broadcasted_iota(jnp.int32, (1, 256), 1)
        source = lane // 16
        local = lane % 4
        first = jnp.zeros((1, 256), jnp.int32)
        kept = jnp.zeros((1, 256), jnp.int32)
        place = jnp.zeros((1, 256), jnp.int32)
        begin = jnp.int32(0)
        for s in range(SHARDS):
            first = jnp.where(source == s, begin, first)
            kept = jnp.where(source == s, count[s], kept)
            begin = begin + count[s]
            for slot in range(KMAX):
                place = jnp.where(
                    (source == s) & (local == slot), pos[s * 16 + order[s, slot]], place
                )
        target = jnp.where(local < kept, first + local, -1)
        listed = lax.broadcasted_iota(jnp.int32, (KEEP, 256), 0) == target
        group = (lane // 4) % 4
        picks = [
            jnp.where(listed & (group == g), 1.0, 0.0).astype(jnp.bfloat16) for g in range(GROUPS)
        ]
        mine = jnp.where(listed & (group == 0), 1.0, 0.0)
        upper = jnp.sum(mine * (place >> 10).astype(jnp.float32), axis=1, keepdims=True)
        lower = jnp.sum(mine * (place & 1023).astype(jnp.float32), axis=1, keepdims=True)
        angle = lower * table[0:1, :] + upper * table[1:2, :]
        return picks, upper * 1024.0 + lower, jnp.cos(angle), jnp.sin(angle) * table[2:3, :]

    def transpose(g):
        at = (KVH + g) * HD
        values_t[g] = cache_v[:, at : at + HD].T

    row_sent, row_arrived, row_pass = relay(slots, row_send, row_recv)
    for at in (5, 6, 7):
        loads[at].wait()
    picks, places, cosine, sine = tables()
    loads[3].wait()
    filler = 0
    for dz, dy in ((0, 1), (1, 0), (3, 0), (2, 0), (1, 1), (3, 1), (2, 1)):
        row_pass(dz, dy)
        transpose(filler)
        filler += 1
    transpose(filler)
    for dy in (0, 1):
        for dz in (0, 1, 3, 2):
            row_arrived(dz, dy, 1)
    loads[1].wait()
    loads[2].wait()
    query = jnp.zeros((KEEP, 4 * HD), jnp.float32)
    keyval = jnp.zeros((KEEP, HD), jnp.float32)
    for g in range(GROUPS):
        rows = contract(picks[g], slots[...].reshape(256, WIDE), (1, 0)).astype(jnp.bfloat16)
        query += contract(rows, query_v[g * WIDE : (g + 1) * WIDE, :], (1, 0))
        keyval += contract(rows, keyval_v[g * WIDE : (g + 1) * WIDE, :], (1, 0))

    def turn(part):
        return part * cosine + pltpu.roll(part, HD // 2, 1) * sine

    for h in range(4):
        qbuf[me, h * KEEP : (h + 1) * KEEP, :] = turn(query[:, h * HD : (h + 1) * HD]).astype(
            jnp.bfloat16
        )
    plain = keyval.astype(jnp.bfloat16).astype(jnp.float32)
    qbuf[me, QROWS:, :] = jnp.where(me < KVH, turn(plain), plain).astype(jnp.bfloat16)

    q_sent, q_arrived, q_pass = relay(qbuf, q_send, q_recv)

    def attend(g):
        keys = cache_v[:, pl.ds(pl.multiple_of(g * HD, HD), HD)]
        both = jnp.concatenate(
            [qbuf[2 * g + 1 - c, :QROWS, :], qbuf[2 * g + c, :QROWS, :]], axis=0
        )
        scores = contract(keys, both, (1, 1))
        top = jnp.max(scores, axis=0, keepdims=True)
        weights = jnp.exp2((scores - top) * EXP2_SCALE)
        total = jnp.sum(weights, axis=0, keepdims=True)
        numer = contract(values_t[g], weights.astype(jnp.bfloat16), (1, 0))
        partial = numer * (1.0 / total)
        lse = top * EXP2_SCALE + jnp.log2(total)
        pack(send_s, g, partial[:, :QROWS], lse[:, :QROWS])
        own[g] = partial[:, QROWS:]
        own_lse[g] = jnp.broadcast_to(lse[:, QROWS:], (8, QROWS))

    def move(src, dst, index_from, index_to, ssem, rsem, peer):
        return pltpu.make_async_remote_copy(
            src_ref=src.at[index_from],
            dst_ref=dst.at[index_to],
            send_sem=ssem,
            recv_sem=rsem,
            device_id={"ctx": peer},
            device_id_type=MESH,
        )

    def to_sibling(dz, dy):
        g = z_at(dz) * 2 + (y if dy == 0 else 1 - y)
        at = dz * 2 + dy
        return move(send_s, recv_s, g, g, s_send.at[at], s_recv.at[at], sibling)

    def to_y(dz):
        return move(send_y, recv_y, dz, dz, y_send.at[dz], y_recv.at[dz], y_peer)

    def to_z(dz):
        return move(send_z, recv_z, dz, ZS - dz, z_send.at[dz], z_recv.at[ZS - dz], z_peer(dz))

    def mine_and_sibling(dz, dy):
        g = z_at(dz) * 2 + (y if dy == 0 else 1 - y)
        to_sibling(dz, dy).wait_recv()
        return [(own[g], own_lse[g, 0:1, :]), unpack(recv_s, g)]

    turns = [(dz, dy) for dz in range(ZS) for dy in (0, 1)]
    passes = {0: ((0, 1), (1, 0), (3, 0)), 1: ((2, 0),), 3: ((1, 1), (3, 1), (2, 1))}

    def follow(dz, dy):
        if dy == 1:
            pack(send_y, dz, *merge(mine_and_sibling(dz, 1)))
            to_y(dz).start()
            return None
        pieces = mine_and_sibling(dz, 0)
        to_y(dz).wait_recv()
        pieces.append(unpack(recv_y, dz))
        if dz == 0:
            return merge(pieces)
        pack(send_z, dz, *merge(pieces))
        to_z(dz).start()
        return None

    def fresh_keys():
        new_keys = qbuf[me // 2, QROWS:, :]
        new_values = qbuf[KVH + me // 2, QROWS:, :]
        spot = lax.broadcasted_iota(jnp.int32, (KEEP, QROWS), 0)
        lane = lax.broadcasted_iota(jnp.int32, (KEEP, QROWS), 1)
        asker = jnp.sum(jnp.where(lane % KEEP == spot, places, 0.0), axis=0, keepdims=True)
        scores = contract(new_keys, qbuf[me, :QROWS, :], (1, 1))
        seen = places <= asker
        scores = jnp.where(seen, scores, -1e30)
        top = jnp.max(scores, axis=0, keepdims=True)
        weights = jnp.where(seen, jnp.exp2((scores - top) * EXP2_SCALE), 0.0)
        total = jnp.sum(weights, axis=0, keepdims=True)
        numer = contract(new_values, weights.astype(jnp.bfloat16), (0, 0))
        fresh = (numer * (1.0 / total), top * EXP2_SCALE + jnp.log2(total))
        return fresh

    local = None
    fresh = None
    attended = 0
    for dz, dy, done in SCHEDULE:
        if done:
            local = follow(dz, dy)
            continue
        for link in passes.get(attended, ()):
            q_pass(*link)
        q_arrived(dz, dy, 1)
        attend(z_at(dz) * 2 + (y if dy == 0 else 1 - y))
        to_sibling(dz, dy).start()
        attended += 1
        if attended == KVH:
            fresh = fresh_keys()

    pieces = [local, fresh]
    for dz in (1, 3, 2):
        pltpu.make_async_remote_copy(
            src_ref=send_z.at[dz],
            dst_ref=recv_z.at[dz],
            send_sem=z_send.at[dz],
            recv_sem=z_recv.at[dz],
            device_id={"ctx": z_peer(dz)},
            device_id_type=MESH,
        ).wait_recv()
        pieces.append(unpack(recv_z, dz))
    mixed, _ = merge(pieces)
    final = mixed.T
    for h in range(4):
        out[:, h * HD : (h + 1) * HD] = final[h * KEEP : (h + 1) * KEEP, :].astype(jnp.bfloat16)

    for copy in row_sent + q_sent:
        copy.wait_send()
    for dz, dy in turns:
        to_sibling(dz, dy).wait_send()
    for dz in range(ZS):
        to_y(dz).wait_send()
    for dz in (1, 2, 3):
        to_z(dz).wait_send()


def kernel_body(hidden, keep_order, keep_count, positions, w_query, w_keyval, cache):
    scaled, wrapped = rope_table(HD)
    sign = jnp.asarray([-1.0] * (HD // 2) + [1.0] * (HD // 2), jnp.float32)
    table = jnp.stack(
        [jnp.concatenate([scaled, scaled]), jnp.concatenate([wrapped, wrapped]), sign]
        + [jnp.zeros((HD,), jnp.float32)] * 5
    )
    vmem = pl.BlockSpec(memory_space=pltpu.VMEM)
    hbm = pl.BlockSpec(memory_space=pltpu.HBM)
    tokens = cache.shape[0]
    bf16 = jnp.bfloat16
    dma = pltpu.SemaphoreType.DMA
    return pl.pallas_call(
        kernel,
        out_shape=jax.ShapeDtypeStruct((KEEP, 4 * HD), bf16),
        in_specs=[hbm] * 8,
        out_specs=vmem,
        scratch_shapes=[
            pltpu.SMEM(keep_order.shape, jnp.int32),
            pltpu.SMEM(keep_count.shape, jnp.int32),
            pltpu.SMEM(positions.shape, jnp.int32),
            pltpu.VMEM(table.shape, jnp.float32),
            pltpu.VMEM(hidden.shape, bf16),
            pltpu.VMEM(w_query.shape, bf16),
            pltpu.VMEM(w_keyval.shape, bf16),
            pltpu.VMEM(cache.shape, bf16),
            pltpu.VMEM((SHARDS, 16, WIDE), bf16),
            pltpu.VMEM((SHARDS, QROWS + KEEP, HD), bf16),
            pltpu.VMEM((KVH, HD, tokens), bf16),
            pltpu.VMEM((KVH, HD, QROWS), jnp.float32),
            pltpu.VMEM((KVH, 8, QROWS), jnp.float32),
            pltpu.VMEM((KVH, MSG, QROWS), bf16),
            pltpu.VMEM((KVH, MSG, QROWS), bf16),
            pltpu.VMEM((ZS, MSG, QROWS), bf16),
            pltpu.VMEM((ZS, MSG, QROWS), bf16),
            pltpu.VMEM((ZS, MSG, QROWS), bf16),
            pltpu.VMEM((ZS, MSG, QROWS), bf16),
            dma((8,)),
            dma((15,)),
            dma((16,)),
            dma((15,)),
            dma((16,)),
            dma((8,)),
            dma((8,)),
            dma((4,)),
            dma((4,)),
            dma((4,)),
            dma((4,)),
        ],
        compiler_params=pltpu.CompilerParams(
            collective_id=0, has_side_effects=True, vmem_limit_bytes=64 * 1024 * 1024 - 64 * 1024
        ),
        cost_estimate=pl.CostEstimate(
            flops=1_500_000_000, bytes_accessed=15_000_000, transcendentals=2_100_000
        ),
    )(keep_order, keep_count, positions, table, hidden, w_query, w_keyval, cache)


def solution(mesh):
    use = kernel_body if mesh.shape["ctx"] == 16 else body
    return jax.shard_map(
        use,
        mesh=mesh,
        in_specs=(
            P(("req", "ctx"), None),
            P("req", None),
            P("req"),
            P("req"),
            P(None, "ctx"),
            P(None, "ctx"),
            P(("req", "ctx"), None),
        ),
        out_specs=P("req", "ctx"),
        check_vma=False,
    )
```

```python
import functools
import math

import jax
import jax.numpy as jnp
from jax import lax
from jax.experimental import pallas as pl
from jax.experimental.pallas import tpu as pltpu
from jax.sharding import PartitionSpec as P

H = 64
KVH = 8
HD = 128
KEEP_DEV = 2
KMAX = 4


def rope_table(head_size):
    half = head_size // 2
    period = 2.0 * math.pi
    scaled_list = []
    wrapped_list = []
    for column in range(half):
        inverse = 500000.0 ** (-2.0 * column / head_size)
        wavelen = 2.0 * math.pi / inverse
        if wavelen > 8192.0:
            scaled_rate = inverse / 8.0
        elif wavelen < 2048.0:
            scaled_rate = inverse
        else:
            smooth = (8192.0 / wavelen - 1.0) / 3.0
            scaled_rate = (1.0 - smooth) * inverse / 8.0 + smooth * inverse
        scaled_list.append(scaled_rate)
        step_angle = 1024.0 * scaled_rate
        wrapped_list.append(step_angle - period * (step_angle // period))
    return (jnp.asarray(scaled_list, jnp.float32), jnp.asarray(wrapped_list, jnp.float32))


def rotate(values, places):
    scaled, wrapped = rope_table(values.shape[-1])
    upper = (places // 1024).astype(jnp.float32)
    lower = (places % 1024).astype(jnp.float32)
    angle = lower[:, None] * scaled[None, :] + upper[:, None] * wrapped[None, :]
    cosine = jnp.cos(angle)[:, None, :]
    sine = jnp.sin(angle)[:, None, :]
    half = values.shape[-1] // 2
    first = values[..., :half]
    second = values[..., half:]
    return jnp.concatenate(
        [first * cosine - second * sine, second * cosine + first * sine], axis=-1
    )


def kept_sources(keep_count, kept_total, shards):
    ends = jnp.cumsum(keep_count)
    starts = ends - keep_count
    slots = jnp.arange(kept_total, dtype=jnp.int32)
    owner = jnp.sum((ends[None, :] <= slots[:, None]).astype(jnp.int32), axis=1)
    ids = jnp.arange(shards, dtype=jnp.int32)
    first = jnp.sum(jnp.where(ids[None, :] == owner[:, None], starts[None, :], 0), axis=1)
    return (owner, slots - first)


def body(hidden, keep_order, keep_count, positions, w_query, w_keyval, cache):
    shards = lax.axis_size("ctx")
    me = lax.axis_index("ctx")
    span_rows = hidden.shape[0]
    kept_total = KEEP_DEV * shards
    block = KEEP_DEV
    cache_rows = cache.shape[0]
    heads_here = H // shards
    order_here = lax.dynamic_slice_in_dim(keep_order, me, 1, 0)[0, :KMAX]
    slot_rows = hidden[order_here]
    rows_all = lax.all_gather(slot_rows, "ctx", axis=0, tiled=True)
    owner, local = kept_sources(keep_count, kept_total, shards)
    rows = rows_all[owner * KMAX + local]
    places = positions[owner * span_rows + keep_order[owner, local]]
    query = jnp.dot(rows, w_query, preferred_element_type=jnp.float32).reshape(
        kept_total, heads_here, HD
    )
    query = rotate(query, places).astype(jnp.bfloat16).reshape(kept_total, heads_here * HD)
    key_part = jnp.dot(rows, w_keyval, preferred_element_type=jnp.float32).astype(jnp.bfloat16)
    own_keyval = lax.all_to_all(key_part, "ctx", split_axis=0, concat_axis=1, tiled=True)
    own_places = lax.dynamic_slice_in_dim(places, me * block, block, 0)
    new_keys = rotate(
        own_keyval[:, : KVH * HD].astype(jnp.float32).reshape(block, KVH, HD), own_places
    )
    new_keys = new_keys.astype(jnp.bfloat16).reshape(block, KVH * HD)
    keys = jnp.concatenate([cache[:, : KVH * HD], new_keys], axis=0)
    values = jnp.concatenate([cache[:, KVH * HD :], own_keyval[:, KVH * HD :]], axis=0)
    queries = lax.all_gather(query, "ctx", axis=1, tiled=True)
    visible = jnp.concatenate(
        [jnp.ones((kept_total, cache_rows), bool), own_places[None, :] <= places[:, None]], axis=1
    )
    group = H // KVH
    scale = 1.0 / math.sqrt(HD)
    numer_list = []
    top_list = []
    total_list = []
    for index in range(KVH):
        q_group = queries[:, index * group * HD : (index + 1) * group * HD].reshape(
            kept_total, group, HD
        )
        k_group = keys[:, index * HD : (index + 1) * HD]
        v_group = values[:, index * HD : (index + 1) * HD]
        scores = (
            jnp.einsum("qhd,kd->qhk", q_group, k_group, preferred_element_type=jnp.float32) * scale
        )
        scores = jnp.where(visible[:, None, :], scores, -1e30)
        top = jnp.max(scores, axis=2)
        weights = jnp.exp(scores - top[..., None])
        total_list.append(jnp.sum(weights, axis=2))
        top_list.append(top)
        numer = jnp.einsum(
            "qhk,kd->qhd", weights.astype(jnp.bfloat16), v_group, preferred_element_type=jnp.float32
        )
        numer_list.append(numer.reshape(kept_total, group * HD))
    numer = jnp.concatenate(numer_list, axis=1)
    top = jnp.concatenate(top_list, axis=1)
    total = jnp.concatenate(total_list, axis=1)
    best = lax.pmax(top.astype(jnp.bfloat16), "ctx").astype(top.dtype)
    factor = jnp.exp(top - best)
    scaled_numer = (numer.reshape(kept_total, H, HD) * factor[..., None]).reshape(
        kept_total, H * HD
    )
    result, denom = (
        lax.psum_scatter(scaled_numer, "ctx", scatter_dimension=1, tiled=True),
        lax.psum_scatter(total * factor, "ctx", scatter_dimension=1, tiled=True),
    )
    result = result.reshape(kept_total, heads_here, HD)
    return (result / denom[..., None]).reshape(kept_total, heads_here * HD).astype(jnp.bfloat16)


MESH = pl.DeviceIdType.MESH
ZS = 4
SHARDS = 16
KEEP = 32
GROUPS = 4
WIDE = 2048
QROWS = 128
SCHEDULE = (
    (0, 1, 0),
    (1, 0, 0),
    (3, 0, 0),
    (1, 1, 0),
    (3, 1, 0),
    (0, 1, 1),
    (2, 1, 0),
    (1, 1, 1),
    (2, 0, 0),
    (3, 1, 1),
    (0, 0, 0),
    (2, 1, 1),
    (1, 0, 1),
    (3, 0, 1),
    (2, 0, 1),
    (0, 0, 1),
)
EXP2_SCALE = math.log2(math.e) / math.sqrt(HD)
MSG = QROWS + 16


def pack(ref, index, partial, lse):
    ref[index, :QROWS, :] = partial.astype(jnp.bfloat16)
    high = lse.astype(jnp.bfloat16).astype(jnp.float32)
    middle = (lse - high).astype(jnp.bfloat16).astype(jnp.float32)
    low = lse - high - middle
    row = lax.broadcasted_iota(jnp.int32, (16, QROWS), 0)
    stats = jnp.where(row == 0, high, jnp.where(row == 1, middle, jnp.where(row == 2, low, 0.0)))
    ref[index, QROWS:, :] = stats.astype(jnp.bfloat16)


def unpack(ref, index):
    stats = ref[index, QROWS:, :].astype(jnp.float32)
    return ref[index, :QROWS, :].astype(jnp.float32), jnp.sum(stats, axis=0, keepdims=True)


def merge(pieces):
    best = functools.reduce(jnp.maximum, [lse for _, lse in pieces])
    factors = [jnp.exp2(lse - best) for _, lse in pieces]
    total = sum(factors)
    inverse = 1.0 / total
    mixed = sum(partial * (factor * inverse) for (partial, _), factor in zip(pieces, factors))
    return mixed, best + jnp.log2(total)


def contract(a, b, dims):
    return lax.dot_general(a, b, ((dims[:1], dims[1:]), ((), ())), preferred_element_type=jnp.float32)


def kernel(
    order_h, count_h, pos_h, table_h, hidden, w_query, w_keyval, cache, out,
    order, count, pos, table, hidden_v, query_v, keyval_v, cache_v, slots, qbuf, values_t,
    own, own_lse, send_s, recv_s, send_y, recv_y, send_z, recv_z,
    load_sem, row_send, row_recv, q_send, q_recv,
    s_send, s_recv, y_send, y_recv, z_send, z_recv,
):
    me = lax.axis_index("ctx")
    z = me // 4
    y = (me // 2) % 2
    c = me % 2
    sibling = me + 1 - 2 * c
    y_peer = me + 2 - 4 * y

    def z_at(dz):
        return (z + dz) % ZS

    def z_peer(dz):
        return z_at(dz) * 4 + me % 4

    def block_at(dz, dy, dc):
        yy = y if dy == 0 else 1 - y
        cc = c if dc == 0 else 1 - c
        return z_at(dz) * 4 + yy * 2 + cc

    loads = [
        pltpu.make_async_copy(hidden, hidden_v, load_sem.at[0]),
        pltpu.make_async_copy(w_query, query_v, load_sem.at[1]),
        pltpu.make_async_copy(w_keyval, keyval_v, load_sem.at[2]),
        pltpu.make_async_copy(cache, cache_v, load_sem.at[3]),
        pltpu.make_async_copy(order_h, order, load_sem.at[4]),
        pltpu.make_async_copy(count_h, count, load_sem.at[5]),
        pltpu.make_async_copy(pos_h, pos, load_sem.at[6]),
        pltpu.make_async_copy(table_h, table, load_sem.at[7]),
    ]
    for at in (4, 0, 5, 6, 7, 3, 1, 2):
        loads[at].start()

    barrier = pltpu.get_barrier_semaphore()
    peers = [sibling, y_peer] + [z_peer(dz) for dz in (1, 2, 3)]
    for peer in peers:
        pl.semaphore_signal(barrier, inc=1, device_id={"ctx": peer}, device_id_type=MESH)

    loads[4].wait()
    row = lax.broadcasted_iota(jnp.int32, (16, 16), 0)
    column = lax.broadcasted_iota(jnp.int32, (16, 16), 1)
    chosen = jnp.zeros((16, 16), jnp.int32)
    for slot in range(KMAX):
        chosen = jnp.where(row % 4 == slot, order[me, slot], chosen)
    loads[0].wait()
    picked = jnp.zeros((16, WIDE), jnp.float32)
    for g in range(GROUPS):
        onehot = jnp.where((chosen == column) & (row // 4 == g), 1.0, 0.0).astype(jnp.bfloat16)
        picked += contract(onehot, hidden_v[:, g * WIDE : (g + 1) * WIDE], (1, 0))
    slots[me] = picked.astype(jnp.bfloat16)
    pl.semaphore_wait(barrier, len(peers))

    def relay(buf, send_sem, recv_sem):
        sent = []

        def send(at, receiver_at, peer):
            copy = pltpu.make_async_remote_copy(
                src_ref=buf.at[block_at(*at)],
                dst_ref=buf.at[block_at(*at)],
                send_sem=send_sem.at[len(sent)],
                recv_sem=recv_sem.at[receiver_at],
                device_id={"ctx": peer},
                device_id_type=MESH,
            )
            copy.start()
            sent.append(copy)

        def arrived(dz, dy, dc):
            pltpu.make_async_remote_copy(
                src_ref=buf.at[block_at(dz, dy, dc)],
                dst_ref=buf.at[block_at(dz, dy, dc)],
                send_sem=send_sem.at[0],
                recv_sem=recv_sem.at[dz * 4 + dy * 2 + dc],
                device_id={"ctx": sibling},
                device_id_type=MESH,
            ).wait_recv()

        def pass_on(dz, dy):
            arrived(dz, dy, 0)
            if dy == 0:
                send((dz, 0, 0), dz * 4 + 2, y_peer)
            send((dz, dy, 0), dz * 4 + dy * 2 + 1, sibling)

        send((0, 0, 0), 2, y_peer)
        send((0, 0, 0), 1, sibling)
        for dz in (1, 3, 2):
            send((0, 0, 0), (ZS - dz) * 4, z_peer(dz))
        return sent, arrived, pass_on

    def tables():
        lane = lax.broadcasted_iota(jnp.int32, (1, 256), 1)
        source = lane // 16
        local = lane % 4
        first = jnp.zeros((1, 256), jnp.int32)
        kept = jnp.zeros((1, 256), jnp.int32)
        place = jnp.zeros((1, 256), jnp.int32)
        begin = jnp.int32(0)
        for s in range(SHARDS):
            first = jnp.where(source == s, begin, first)
            kept = jnp.where(source == s, count[s], kept)
            begin = begin + count[s]
            for slot in range(KMAX):
                place = jnp.where(
                    (source == s) & (local == slot), pos[s * 16 + order[s, slot]], place
                )
        target = jnp.where(local < kept, first + local, -1)
        listed = lax.broadcasted_iota(jnp.int32, (KEEP, 256), 0) == target
        group = (lane // 4) % 4
        picks = [
            jnp.where(listed & (group == g), 1.0, 0.0).astype(jnp.bfloat16) for g in range(GROUPS)
        ]
        mine = jnp.where(listed & (group == 0), 1.0, 0.0)
        upper = jnp.sum(mine * (place >> 10).astype(jnp.float32), axis=1, keepdims=True)
        lower = jnp.sum(mine * (place & 1023).astype(jnp.float32), axis=1, keepdims=True)
        angle = lower * table[0:1, :] + upper * table[1:2, :]
        return picks, upper * 1024.0 + lower, jnp.cos(angle), jnp.sin(angle) * table[2:3, :]

    def transpose(g):
        at = (KVH + g) * HD
        values_t[g] = cache_v[:, at : at + HD].T

    row_sent, row_arrived, row_pass = relay(slots, row_send, row_recv)
    for at in (5, 6, 7):
        loads[at].wait()
    picks, places, cosine, sine = tables()
    loads[3].wait()
    filler = 0
    for dz, dy in ((0, 1), (1, 0), (3, 0), (2, 0), (1, 1), (3, 1), (2, 1)):
        row_pass(dz, dy)
        transpose(filler)
        filler += 1
    transpose(filler)
    for dy in (0, 1):
        for dz in (0, 1, 3, 2):
            row_arrived(dz, dy, 1)
    loads[1].wait()
    loads[2].wait()
    query = jnp.zeros((KEEP, 4 * HD), jnp.float32)
    keyval = jnp.zeros((KEEP, HD), jnp.float32)
    for g in range(GROUPS):
        rows = contract(picks[g], slots[...].reshape(256, WIDE), (1, 0)).astype(jnp.bfloat16)
        query += contract(rows, query_v[g * WIDE : (g + 1) * WIDE, :], (1, 0))
        keyval += contract(rows, keyval_v[g * WIDE : (g + 1) * WIDE, :], (1, 0))

    def turn(part):
        return part * cosine + pltpu.roll(part, HD // 2, 1) * sine

    for h in range(4):
        qbuf[me, h * KEEP : (h + 1) * KEEP, :] = turn(query[:, h * HD : (h + 1) * HD]).astype(
            jnp.bfloat16
        )
    plain = keyval.astype(jnp.bfloat16).astype(jnp.float32)
    qbuf[me, QROWS:, :] = jnp.where(me < KVH, turn(plain), plain).astype(jnp.bfloat16)

    q_sent, q_arrived, q_pass = relay(qbuf, q_send, q_recv)

    def attend(g):
        keys = cache_v[:, pl.ds(pl.multiple_of(g * HD, HD), HD)]
        both = jnp.concatenate(
            [qbuf[2 * g + 1 - c, :QROWS, :], qbuf[2 * g + c, :QROWS, :]], axis=0
        )
        scores = contract(keys, both, (1, 1))
        top = jnp.max(scores, axis=0, keepdims=True)
        weights = jnp.exp2((scores - top) * EXP2_SCALE)
        total = jnp.sum(weights, axis=0, keepdims=True)
        numer = contract(values_t[g], weights.astype(jnp.bfloat16), (1, 0))
        partial = numer * (1.0 / total)
        lse = top * EXP2_SCALE + jnp.log2(total)
        pack(send_s, g, partial[:, :QROWS], lse[:, :QROWS])
        own[g] = partial[:, QROWS:]
        own_lse[g] = jnp.broadcast_to(lse[:, QROWS:], (8, QROWS))

    def move(src, dst, index_from, index_to, ssem, rsem, peer):
        return pltpu.make_async_remote_copy(
            src_ref=src.at[index_from],
            dst_ref=dst.at[index_to],
            send_sem=ssem,
            recv_sem=rsem,
            device_id={"ctx": peer},
            device_id_type=MESH,
        )

    def to_sibling(dz, dy):
        g = z_at(dz) * 2 + (y if dy == 0 else 1 - y)
        at = dz * 2 + dy
        return move(send_s, recv_s, g, g, s_send.at[at], s_recv.at[at], sibling)

    def to_y(dz):
        return move(send_y, recv_y, dz, dz, y_send.at[dz], y_recv.at[dz], y_peer)

    def to_z(dz):
        return move(send_z, recv_z, dz, ZS - dz, z_send.at[dz], z_recv.at[ZS - dz], z_peer(dz))

    def mine_and_sibling(dz, dy):
        g = z_at(dz) * 2 + (y if dy == 0 else 1 - y)
        to_sibling(dz, dy).wait_recv()
        return [(own[g], own_lse[g, 0:1, :]), unpack(recv_s, g)]

    turns = [(dz, dy) for dz in range(ZS) for dy in (0, 1)]
    passes = {0: ((0, 1), (1, 0), (3, 0), (2, 0)), 3: ((1, 1), (3, 1), (2, 1))}

    def follow(dz, dy):
        if dy == 1:
            pack(send_y, dz, *merge(mine_and_sibling(dz, 1)))
            to_y(dz).start()
            return None
        pieces = mine_and_sibling(dz, 0)
        to_y(dz).wait_recv()
        pieces.append(unpack(recv_y, dz))
        if dz == 0:
            return merge(pieces)
        pack(send_z, dz, *merge(pieces))
        to_z(dz).start()
        return None

    def fresh_keys():
        new_keys = qbuf[me // 2, QROWS:, :]
        new_values = qbuf[KVH + me // 2, QROWS:, :]
        spot = lax.broadcasted_iota(jnp.int32, (KEEP, QROWS), 0)
        lane = lax.broadcasted_iota(jnp.int32, (KEEP, QROWS), 1)
        asker = jnp.sum(jnp.where(lane % KEEP == spot, places, 0.0), axis=0, keepdims=True)
        scores = contract(new_keys, qbuf[me, :QROWS, :], (1, 1))
        seen = places <= asker
        scores = jnp.where(seen, scores, -1e30)
        top = jnp.max(scores, axis=0, keepdims=True)
        weights = jnp.where(seen, jnp.exp2((scores - top) * EXP2_SCALE), 0.0)
        total = jnp.sum(weights, axis=0, keepdims=True)
        numer = contract(new_values, weights.astype(jnp.bfloat16), (0, 0))
        fresh = (numer * (1.0 / total), top * EXP2_SCALE + jnp.log2(total))
        return fresh

    local = None
    fresh = None
    attended = 0
    for dz, dy, done in SCHEDULE:
        if done:
            local = follow(dz, dy)
            continue
        for link in passes.get(attended, ()):
            q_pass(*link)
        q_arrived(dz, dy, 1)
        attend(z_at(dz) * 2 + (y if dy == 0 else 1 - y))
        to_sibling(dz, dy).start()
        attended += 1
        if attended == KVH:
            fresh = fresh_keys()

    pieces = [local, fresh]
    for dz in (1, 3, 2):
        pltpu.make_async_remote_copy(
            src_ref=send_z.at[dz],
            dst_ref=recv_z.at[dz],
            send_sem=z_send.at[dz],
            recv_sem=z_recv.at[dz],
            device_id={"ctx": z_peer(dz)},
            device_id_type=MESH,
        ).wait_recv()
        pieces.append(unpack(recv_z, dz))
    mixed, _ = merge(pieces)
    final = mixed.T
    for h in range(4):
        out[:, h * HD : (h + 1) * HD] = final[h * KEEP : (h + 1) * KEEP, :].astype(jnp.bfloat16)

    for copy in row_sent + q_sent:
        copy.wait_send()
    for dz, dy in turns:
        to_sibling(dz, dy).wait_send()
    for dz in range(ZS):
        to_y(dz).wait_send()
    for dz in (1, 2, 3):
        to_z(dz).wait_send()


def kernel_body(hidden, keep_order, keep_count, positions, w_query, w_keyval, cache):
    scaled, wrapped = rope_table(HD)
    sign = jnp.asarray([-1.0] * (HD // 2) + [1.0] * (HD // 2), jnp.float32)
    table = jnp.stack(
        [jnp.concatenate([scaled, scaled]), jnp.concatenate([wrapped, wrapped]), sign]
        + [jnp.zeros((HD,), jnp.float32)] * 5
    )
    vmem = pl.BlockSpec(memory_space=pltpu.VMEM)
    hbm = pl.BlockSpec(memory_space=pltpu.HBM)
    tokens = cache.shape[0]
    bf16 = jnp.bfloat16
    dma = pltpu.SemaphoreType.DMA
    return pl.pallas_call(
        kernel,
        out_shape=jax.ShapeDtypeStruct((KEEP, 4 * HD), bf16),
        in_specs=[hbm] * 8,
        out_specs=vmem,
        scratch_shapes=[
            pltpu.SMEM(keep_order.shape, jnp.int32),
            pltpu.SMEM(keep_count.shape, jnp.int32),
            pltpu.SMEM(positions.shape, jnp.int32),
            pltpu.VMEM(table.shape, jnp.float32),
            pltpu.VMEM(hidden.shape, bf16),
            pltpu.VMEM(w_query.shape, bf16),
            pltpu.VMEM(w_keyval.shape, bf16),
            pltpu.VMEM(cache.shape, bf16),
            pltpu.VMEM((SHARDS, 16, WIDE), bf16),
            pltpu.VMEM((SHARDS, QROWS + KEEP, HD), bf16),
            pltpu.VMEM((KVH, HD, tokens), bf16),
            pltpu.VMEM((KVH, HD, QROWS), jnp.float32),
            pltpu.VMEM((KVH, 8, QROWS), jnp.float32),
            pltpu.VMEM((KVH, MSG, QROWS), bf16),
            pltpu.VMEM((KVH, MSG, QROWS), bf16),
            pltpu.VMEM((ZS, MSG, QROWS), bf16),
            pltpu.VMEM((ZS, MSG, QROWS), bf16),
            pltpu.VMEM((ZS, MSG, QROWS), bf16),
            pltpu.VMEM((ZS, MSG, QROWS), bf16),
            dma((8,)),
            dma((15,)),
            dma((16,)),
            dma((15,)),
            dma((16,)),
            dma((8,)),
            dma((8,)),
            dma((4,)),
            dma((4,)),
            dma((4,)),
            dma((4,)),
        ],
        compiler_params=pltpu.CompilerParams(
            collective_id=0, has_side_effects=True, vmem_limit_bytes=64 * 1024 * 1024 - 64 * 1024
        ),
        cost_estimate=pl.CostEstimate(
            flops=1_500_000_000, bytes_accessed=15_000_000, transcendentals=2_100_000
        ),
    )(keep_order, keep_count, positions, table, hidden, w_query, w_keyval, cache)


def solution(mesh):
    use = kernel_body if mesh.shape["ctx"] == 16 else body
    return jax.shard_map(
        use,
        mesh=mesh,
        in_specs=(
            P(("req", "ctx"), None),
            P("req", None),
            P("req"),
            P("req"),
            P(None, "ctx"),
            P(None, "ctx"),
            P(("req", "ctx"), None),
        ),
        out_specs=P("req", "ctx"),
        check_vma=False,
    )
```
